256 devices in a mesh: space: 16 (over y_lo, x, core), dp: 16 (over y_hi, z).
Axes of the slice: x: 4, y: 4 (y_hi: 2, y_lo: 2; y = y_hi * 2 + y_lo), z: 8, core: 2. Of those that a mesh axis runs over, the one named last changes fastest.
Arguments:
- deep_grad: bfloat16 [256, 64, 20, 512], P(('dp', 'space')), may hold values from -48 to 48
- deep_weight: bfloat16 [1024, 512], replicated, may hold values from -0.1875 to 0.1875
- pre_first: bfloat16 [256, 64, 20, 256], P('dp', 'space'), may hold values from -6 to 6
- relu_first: bfloat16 [256, 64, 20, 256], P('dp', 'space'), may hold values from 0 to 6
- pre_middle: bfloat16 [256, 64, 20, 256], P('dp', 'space'), may hold values from -6 to 6
- relu_middle: bfloat16 [256, 64, 20, 256], P('dp', 'space'), may hold values from 0 to 6
- pre_last: bfloat16 [256, 64, 20, 1024], P('dp', 'space'), may hold values from -6 to 6
- block_output: bfloat16 [256, 64, 20, 1024], P('dp', 'space'), may hold values from 0 to 6
- weight_middle: bfloat16 [2304, 256], replicated, may hold values from -0.125 to 0.125
- weight_last: bfloat16 [256, 1024], replicated, may hold values from -0.375 to 0.375
- norm_mean: float32 [1536], replicated, may hold values from -3 to 3
- norm_rstd: float32 [1536], replicated, may hold values from 0.5 to 2
- norm_gain: float32 [1536], replicated, may hold values from 0.1 to 1.9
Outputs:
- first_grad: bfloat16 [256, 64, 20, 256], P('dp', 'space')
- weight_grads: float32 [851968], P(('space', 'dp'))
- norm_grads: float32 [2, 1536], replicated
The draws below stay inside these ranges and needn't reach their ends.
All inputs are finite; a program needn't handle non-finite values.
Results may differ from the reference program's by a relative error of at most 0.012.
Values may be sent and summed in bfloat16 or wider, within the bound.
A program may use at most 128 MiB of HBM per device.

```python
import math
import jax
import jax.numpy as jnp
from jax import lax

CH = 1024
MID = 256
MID4 = 512
COLS = 20
ROWS = 64
GROUP = 16
BATCH = 256
N_DP = 16


def draw_deep_grad(key, part):
    key = jax.random.fold_in(key, 11)
    base_key, chan_key = jax.random.split(key)
    shape = (BATCH, ROWS, COLS, MID4)
    heights = jnp.arange(ROWS, dtype=jnp.float32) / max(ROWS - 1, 1)
    base = jnp.clip(jax.random.normal(base_key, shape, jnp.float32), -6.0, 6.0)
    rising = 1.0 + 2.0 * heights
    channel_scale = jnp.exp(jax.random.uniform(chan_key, (MID4,), jnp.float32, 0.0, math.log(4.0)))
    return (0.3 * base * rising[None, :, None, None] * channel_scale).astype(jnp.bfloat16)


def rectified(values):
    return jnp.clip(values, 0.0, 6.0)


def draw_relu_first(key, part):
    key = jax.random.fold_in(key, 21)
    shape = (BATCH, ROWS, COLS, MID)
    values = jax.random.normal(key, shape, jnp.float32)
    return rectified(values).astype(jnp.bfloat16)


def draw_relu_middle(key, part):
    key = jax.random.fold_in(key, 31)
    shape = (BATCH, ROWS, COLS, MID)
    values = jax.random.normal(key, shape, jnp.float32)
    return rectified(values).astype(jnp.bfloat16)


def draw_block_output(key, part):
    key = jax.random.fold_in(key, 41)
    shape = (BATCH, ROWS, COLS, CH)
    values = jax.random.normal(key, shape, jnp.float32)
    return rectified(values).astype(jnp.bfloat16)


def shard_levels(stream_key, dims, shards, smallest, high):
    loudness = 1.0
    for axis_at, parts in shards:
        draws = jax.random.uniform(jax.random.fold_in(jax.random.fold_in(stream_key, 6), axis_at), (parts,), jnp.float32, smallest / len(shards), high / len(shards))
        loudness = loudness * jnp.repeat(jnp.exp(draws), dims[axis_at] // parts).reshape((-1,) + (1,) * (len(dims) - 1 - axis_at))
    return loudness


def centred(stream_key, extent, scale, reach, cuts=(), kind=jnp.bfloat16):
    values = scale * jax.random.normal(stream_key, extent, jnp.float32)
    if cuts:
        values = values * shard_levels(stream_key, extent, cuts, -0.22, 0.18)
    return jnp.clip(values, -reach, reach).astype(kind)


def setup_inputs(seed: int = 0) -> dict:
    key_list = jax.random.split(jax.random.key(seed), 14)
    deep_grad = draw_deep_grad(jax.random.fold_in(key_list[13], 71), 0)
    deep_weight = centred(key_list[1], (CH, MID4), CH ** -0.5, 0.1875)
    pre_first = centred(key_list[2], (BATCH, ROWS, COLS, MID), 1.0, 6.0, ((0, 16), (1, 16)))
    relu_first = draw_relu_first(jax.random.fold_in(key_list[13], 71), 0)
    pre_middle = centred(key_list[4], (BATCH, ROWS, COLS, MID), 1.0, 6.0, ((0, 16), (1, 16)))
    relu_middle = draw_relu_middle(jax.random.fold_in(key_list[13], 71), 0)
    pre_last = centred(key_list[6], (BATCH, ROWS, COLS, CH), 1.0, 6.0, ((0, 16), (1, 16)))
    block_output = draw_block_output(jax.random.fold_in(key_list[13], 71), 0)
    weight_middle = centred(key_list[8], (9 * MID, MID), (9 * MID) ** -0.5, 0.125)
    weight_last = centred(key_list[9], (MID, CH), MID ** -0.5, 0.375)
    norm_mean = centred(key_list[10], (2 * MID + CH,), 0.5, 3.0, (), jnp.float32)
    norm_rstd = jnp.clip(jnp.exp(jax.random.uniform(key_list[11], (2 * MID + CH,), jnp.float32, math.log(0.5), math.log(2.0))), 0.5, 2.0)
    norm_gain = jnp.clip(1.0 + 0.18 * jax.random.normal(key_list[12], (2 * MID + CH,), jnp.float32), 0.1, 1.9)
    return dict(deep_grad=deep_grad, deep_weight=deep_weight, pre_first=pre_first, relu_first=relu_first, pre_middle=pre_middle, relu_middle=relu_middle, pre_last=pre_last, block_output=block_output, weight_middle=weight_middle, weight_last=weight_last, norm_mean=norm_mean, norm_rstd=norm_rstd, norm_gain=norm_gain)


def norm_back(gradient, saved, centre, spread, gains, positions):
    normed = (saved.astype(jnp.float32) - centre) * spread
    totals = lax.optimization_barrier(jnp.sum(gradient, axis=0))
    crossed = lax.optimization_barrier(jnp.sum(gradient * normed, axis=0))
    result = gains * spread * (gradient - totals / positions - normed * crossed / positions)
    return (result.astype(jnp.bfloat16), totals, crossed)

def tap_columns(padded):
    height = padded.shape[1] - 2
    breadth = padded.shape[2] - 2
    pieces = []
    for row_offset in (-1, 0, 1):
        for col_offset in (-1, 0, 1):
            pieces.append(padded[:, 1 - row_offset:1 - row_offset + height, 1 - col_offset:1 - col_offset + breadth, :])
    stacked = jnp.concatenate(pieces, axis=-1)
    return stacked.reshape(-1, stacked.shape[-1])

def reference(deep_grad, deep_weight, pre_first, relu_first, pre_middle, relu_middle, pre_last, block_output, weight_middle, weight_last, norm_mean, norm_rstd, norm_gain):
    positions = float(GROUP * ROWS * COLS)
    factor = 1.0 / math.sqrt(BATCH * ROWS * COLS)
    middle_turned = weight_middle.reshape(9, MID, MID).transpose(0, 2, 1).reshape(9 * MID, MID)

    def one_group(items):
        sample_grad, saved_first, kept_first, saved_middle, kept_middle, saved_last, kept_out = items
        grad_rows = sample_grad.reshape(-1, MID4)
        upstream = jnp.dot(grad_rows, deep_weight.T, preferred_element_type=jnp.float32).astype(jnp.bfloat16)
        outer = jnp.where(kept_out.reshape(-1, CH) > 0, upstream.astype(jnp.float32), 0.0)
        last_dz, last_totals, last_crossed = norm_back(outer, saved_last.reshape(-1, CH), norm_mean[2 * MID:], norm_rstd[2 * MID:], norm_gain[2 * MID:], positions)
        middle_flat = kept_middle.reshape(-1, MID)
        middle_in = jnp.where(middle_flat > 0, jnp.dot(last_dz, weight_last.T, preferred_element_type=jnp.float32), 0.0)
        last_sum = jnp.dot(middle_flat.T, last_dz, preferred_element_type=jnp.float32)
        middle_dz, middle_totals, middle_crossed = norm_back(middle_in, saved_middle.reshape(-1, MID), norm_mean[MID:2 * MID], norm_rstd[MID:2 * MID], norm_gain[MID:2 * MID], positions)
        padded = jnp.pad(middle_dz.reshape(GROUP, ROWS, COLS, MID), ((0, 0), (1, 1), (1, 1), (0, 0)))
        columns = tap_columns(padded)
        first_flat = kept_first.reshape(-1, MID)
        first_in = jnp.where(first_flat > 0, jnp.dot(columns, middle_turned, preferred_element_type=jnp.float32), 0.0)
        middle_sum = jnp.dot(first_flat.T, columns, preferred_element_type=jnp.float32)
        middle_sum = middle_sum.reshape(MID, 9, MID).transpose(1, 0, 2).reshape(9 * MID, MID)
        first_dz, first_totals, first_crossed = norm_back(first_in, saved_first.reshape(-1, MID), norm_mean[:MID], norm_rstd[:MID], norm_gain[:MID], positions)
        flat_sums = jnp.concatenate([middle_sum.reshape(-1), last_sum.reshape(-1)])
        moments = jnp.stack([jnp.concatenate([first_crossed, middle_crossed, last_crossed]), jnp.concatenate([first_totals, middle_totals, last_totals])])
        return (first_dz.reshape(GROUP, ROWS, COLS, MID), flat_sums, moments)

    def grouped(array):
        return array.reshape((N_DP, GROUP) + array.shape[1:])
    stacked = lax.map(one_group, (grouped(deep_grad), grouped(pre_first), grouped(relu_first), grouped(pre_middle), grouped(relu_middle), grouped(pre_last), grouped(block_output)))
    first_grad = stacked[0].reshape(BATCH, ROWS, COLS, MID)
    weight_grads = lax.optimization_barrier(jnp.sum(stacked[1], axis=0)) * factor
    norm_grads = lax.optimization_barrier(jnp.sum(stacked[2], axis=0)) * factor
    return (first_grad, weight_grads, norm_grads)
```

```python
import functools
import math

import jax
import jax.numpy as jnp
from jax import lax
from jax.experimental import pallas as pl
from jax.experimental.pallas import tpu as pltpu
from jax.sharding import PartitionSpec as P

MESH = pl.DeviceIdType.MESH
F32 = jnp.float32
BF16 = jnp.bfloat16

NS = 16
ND = 16
GROUP = 16
SLAB = 4
COLS = 20
ROWS = 64
CH = 1024
MID = 256
MID4 = 512
POS = GROUP * SLAB * COLS
PLANE = GROUP * COLS
BLOCK = SLAB * COLS
FLAT = 9 * MID + CH
SHARE = FLAT // NS
PIECE = SHARE // ND
M = float(GROUP * ROWS * COLS)
FACTOR = 1.0 / math.sqrt(M * ND)
NT = (((1,), (1,)), ((), ()))


def folded(values):
    return jnp.sum(values.reshape(-1, 8, values.shape[-1]), axis=0)


def lanes(ref, rows):
    return jnp.concatenate([ref[0, rows, :], ref[1, rows, :]], axis=1)


def kernel(
    dg_hbm, wd_hbm, pf_hbm, rf_hbm, pm_hbm, rm_hbm, pz_hbm, bo_hbm, wm_hbm, wl_hbm,
    mean_ref, rstd_ref, gain_ref,
    out_hbm, wg_ref, ng_ref,
    dgv, send, recv, wd, bo4, pz4, pf4, rf4, pm4, rm4, wl, wcat,
    glast, ldz, zcm, gmid, stage, hstage, buf, rfh, rft, rmt, zfh, gfirst, ob4,
    acc, st1, st2, st3, std,
    zsend, gsend, zhalo, ghalo, masks,
    pflat, part, ra, sb, rb, tc, sc, rc,
    lsem, dsem, osem,
    a2a_s, a2a_r, s1s, s1r, s2s, s2r, s3s, s3r, sds, sdr, hs, hr,
    as_, ar_, bs_, br_, cs_, cr_,
):
    me = lax.axis_index("space")
    dp = lax.axis_index("dp")

    dg_copies = [
        pltpu.make_async_copy(
            dg_hbm.at[:, pl.ds(16 * u, 16), :], dgv.at[:, pl.ds(16 * u, 16), :], dsem.at[u]
        )
        for u in range(4)
    ]
    for copy in dg_copies:
        copy.start()
    loads = []

    def load(src, dst):
        copy = pltpu.make_async_copy(src, dst, lsem.at[len(loads)])
        copy.start()
        loads.append(copy)
        return copy

    def load_tiles(src, dst, count):
        return [load(src.at[:, :, pl.ds(128 * j, 128)], dst.at[j]) for j in range(count)]

    barrier = pltpu.get_barrier_semaphore()

    def greet(k, carry):
        pl.semaphore_signal(
            barrier, inc=1, device_id=(lax.rem(me + k, NS), dp), device_id_type=MESH
        )
        pl.semaphore_signal(
            barrier, inc=1, device_id=(me, lax.rem(dp + k, ND)), device_id_type=MESH
        )
        return carry

    lax.fori_loop(1, NS, greet, 0)

    ld_pm = load_tiles(pm_hbm, pm4, 2)
    ld_rm = load_tiles(rm_hbm, rm4, 2)
    ld_wd = [load(wd_hbm, wd)]
    ld_bo = load_tiles(bo_hbm, bo4, 8)
    ld_pz = load_tiles(pz_hbm, pz4, 8)
    ld_rf = load_tiles(rf_hbm, rf4, 2)
    ld_pf = load_tiles(pf_hbm, pf4, 2)
    ld_wl = [load(wl_hbm, wl)]
    ld_wc = [
        load(wm_hbm.at[pl.ds(t * MID, MID)], wcat.at[t // 3, :, pl.ds((t % 3) * MID, MID)])
        for t in range(9)
    ]

    bo = bo4.reshape(8, POS, 128)
    pz = pz4.reshape(8, POS, 128)
    pf = pf4.reshape(2, POS, 128)
    rf = rf4.reshape(2, POS, 128)
    pm = pm4.reshape(2, POS, 128)
    rm = rm4.reshape(2, POS, 128)
    ob = ob4.reshape(2, POS, 128)

    def exchange(target, sender):
        return pltpu.make_async_remote_copy(
            src_ref=send.at[target],
            dst_ref=recv.at[pl.ds(pl.multiple_of(sender * BLOCK, BLOCK), BLOCK)],
            send_sem=a2a_s.at[target],
            recv_sem=a2a_r.at[sender],
            device_id=(target, dp),
            device_id_type=MESH,
        )

    for copy in dg_copies:
        copy.wait()
    my_group = lax.div(me, 4)

    def pack(step, carry):
        u = lax.rem(my_group + jnp.where(step == 0, 2, jnp.where(step == 1, 1, jnp.where(step == 2, 3, 0))), 4)
        x = dgv[:, pl.ds(pl.multiple_of(u * 16, 16), 16), :].astype(F32)
        low = lax.broadcasted_iota(jnp.int32, (10, 8, MID4), 1) < 4
        for half in range(2):
            y = x[:, 8 * half : 8 * half + 8, :].reshape(10, 2, 8, MID4)
            even, odd = y[:, 0], y[:, 1]
            first = jnp.where(low, even, pltpu.roll(odd, 4, 1))
            second = jnp.where(low, pltpu.roll(even, 4, 1), odd)
            send[u * 4 + 2 * half] = first.reshape(BLOCK, MID4).astype(BF16)
            send[u * 4 + 2 * half + 1] = second.reshape(BLOCK, MID4).astype(BF16)

        @pl.when(step == 0)
        def _():
            pl.semaphore_wait(barrier, NS + ND - 2)

        for q in range(4):
            target = u * 4 + q

            @pl.when(target != me)
            def _():
                exchange(target, me).start()

        return carry

    lax.fori_loop(0, 4, pack, 0)
    recv[pl.ds(pl.multiple_of(me * BLOCK, BLOCK), BLOCK), :] = send[me]

    mean = lambda lo, n: mean_ref[pl.ds(lo, n)].reshape(1, n)
    rstd = lambda lo, n: rstd_ref[pl.ds(lo, n)].reshape(1, n)
    gain = lambda lo, n: gain_ref[pl.ds(lo, n)].reshape(1, n)

    def halo(src, dst, sem, to_up):
        slot = 0 if to_up else 1
        target = lax.rem(me + (NS - 1 if to_up else 1), NS)
        return pltpu.make_async_remote_copy(
            src_ref=src.at[slot],
            dst_ref=dst.at[1 - slot],
            send_sem=hs.at[sem, slot],
            recv_sem=hr.at[sem, 1 - slot],
            device_id=(target, dp),
            device_id_type=MESH,
        )

    def send_halos(src, dst, sem):
        @pl.when(me > 0)
        def _():
            halo(src, dst, sem, True).start()

        @pl.when(me < NS - 1)
        def _():
            halo(src, dst, sem, False).start()

    def wait_halos(src, dst, sem):
        @pl.when(me > 0)
        def _():
            halo(src, dst, sem, True).wait_send()
            halo(src, dst, sem, False).wait_recv()

        @pl.when(me < NS - 1)
        def _():
            halo(src, dst, sem, False).wait_send()
            halo(src, dst, sem, True).wait_recv()

    for copy in ld_pm:
        copy.wait()
    for l in range(2):
        raw = pm[l].astype(F32)
        stage[l, pl.ds(8, POS), :] = raw
        zcm[l] = raw - mean(MID + 128 * l, 128)
    for slot, h in ((0, 0), (1, SLAB - 1)):
        for l in range(2):
            zsend[slot, :, l * 128 : l * 128 + 128] = stage[
                l, pl.ds(8 + h, PLANE, stride=SLAB), :
            ].astype(BF16)
    send_halos(zsend, zhalo, 0)

    for copy in ld_rm:
        copy.wait()
    for l in range(2):
        rmt[pl.ds(l * 128, 128), :] = rm[l].T

    row = lax.broadcasted_iota(jnp.int32, (PLANE, 128), 0)
    column = lax.rem(row, COLS)
    masks[0] = jnp.where(column == COLS - 1, 0.0, 1.0)
    masks[1] = jnp.where(column == 0, 0.0, 1.0)

    for copy in ld_rf:
        copy.wait()
    for l in range(2):
        stage[l, pl.ds(8, POS), :] = rf[l].astype(F32)
    for h in range(SLAB):
        for l in range(2):
            rfh[pl.ds(h * PLANE, PLANE), l * 128 : l * 128 + 128] = stage[
                l, pl.ds(8 + h, PLANE, stride=SLAB), :
            ].astype(BF16)
    for l in range(2):
        rft[pl.ds(l * 128, 128), :] = rfh[:, l * 128 : l * 128 + 128].T

    for copy in ld_pf:
        copy.wait()
    for l in range(2):
        stage[l, pl.ds(8, POS), :] = pf[l].astype(F32)
    for h in range(SLAB):
        for l in range(2):
            zfh[pl.ds(h * PLANE, PLANE), l * 128 : l * 128 + 128] = stage[
                l, pl.ds(8 + h, PLANE, stride=SLAB), :
            ].astype(BF16)
    for l in range(2):
        stage[l, pl.ds(0, 8), :] = jnp.zeros((8, 128), F32)
        stage[l, pl.ds(8 + POS, 8), :] = jnp.zeros((8, 128), F32)
        for side in range(2):
            hstage[side, l, pl.ds(0, 8), :] = jnp.zeros((8, 128), F32)
            hstage[side, l, pl.ds(8 + PLANE, 8), :] = jnp.zeros((8, 128), F32)

    for copy in ld_wd + ld_bo + ld_pz + ld_wl + ld_wc:
        copy.wait()

    acc[...] = jnp.zeros_like(acc)

    def project(step, carry):
        group = lax.rem(my_group + jnp.where(step == 0, 0, jnp.where(step == 1, 2, jnp.where(step == 2, 3, 1))), 4)
        for q in range(4):
            sender = group * 4 + q

            @pl.when(sender != me)
            def _():
                exchange(sender, sender).wait_recv()

        rows = pl.ds(pl.multiple_of(group * PLANE, PLANE), PLANE)
        for c in range(4):
            up = lax.dot_general(
                recv[rows, :], wd[pl.ds(c * 256, 256), :], NT, preferred_element_type=F32
            )
            for l in range(2):
                j = 2 * c + l
                at = slice(j * 128, j * 128 + 128)
                g = up[:, l * 128 : l * 128 + 128].astype(BF16).astype(F32)
                g = jnp.where(bo[j, rows, :].astype(F32) > 0, g, 0.0)
                glast[rows, at] = g.astype(BF16)
                z = pz[j, rows, :].astype(F32) - mean(2 * MID + 128 * j, 128)
                acc[0, :, at] += folded(g)
                acc[1, :, at] += folded(g * z)
        return carry

    lax.fori_loop(0, 4, project, 0)

    def share(slots, own, sends, recvs, axis):
        at = me if axis == "space" else dp

        def desc(other, sender):
            return pltpu.make_async_remote_copy(
                src_ref=slots.at[at],
                dst_ref=slots.at[sender],
                send_sem=sends.at[other],
                recv_sem=recvs.at[sender],
                device_id=(other, dp) if axis == "space" else (me, other),
                device_id_type=MESH,
            )

        slots[at] = own

        def go(k, carry):
            desc(lax.rem(at + k, 16), at).start()
            return carry

        lax.fori_loop(1, 16, go, 0)

        def finish():
            def wait(k, carry):
                other = lax.rem(at + k, 16)
                desc(other, other).wait_recv()
                return carry

            lax.fori_loop(1, 16, wait, 0)
            return jnp.sum(slots[...], axis=0)

        def drain():
            def wait(k, carry):
                desc(lax.rem(at + k, 16), at).wait_send()
                return carry

            lax.fori_loop(1, 16, wait, 0)

        return finish, drain

    def coefficients(sums, lo, n):
        scale = gain(lo, n) * rstd(lo, n)
        crossed = sums[1:2] * rstd(lo, n)
        slope = -scale * rstd(lo, n) * crossed * (1.0 / M)
        shift = -scale * sums[0:1] * (1.0 / M)
        return scale, slope, shift, crossed

    own = jnp.concatenate(
        [jnp.sum(acc[0], axis=0, keepdims=True), jnp.sum(acc[1], axis=0, keepdims=True)], axis=0
    )
    finish1, drain1 = share(st1, own, s1s, s1r, "space")
    sums1 = finish1()
    scale1, slope1, shift1, crossed1 = coefficients(sums1, 2 * MID, CH)
    std[dp, 0:1, 2 * MID :] = crossed1
    std[dp, 1:2, 2 * MID :] = sums1[0:1]

    acc[...] = jnp.zeros_like(acc)
    mean1 = mean(2 * MID, CH)

    def middle(step, carry):
        rows = pl.ds(pl.multiple_of(step * PLANE, PLANE), PLANE)
        for j in range(8):
            at = slice(j * 128, j * 128 + 128)
            z = pz[j, rows, :].astype(F32) - mean1[:, at]
            ldz[rows, at] = (
                glast[rows, at].astype(F32) * scale1[:, at] + z * slope1[:, at] + shift1[:, at]
            ).astype(BF16)
        mi = lax.dot_general(ldz[rows, :], wl[...], NT, preferred_element_type=F32)
        for l in range(2):
            at = slice(l * 128, l * 128 + 128)
            g = jnp.where(rm[l, rows, :].astype(F32) > 0, mi[:, at], 0.0)
            gmid[l, rows, :] = g
            acc[0, :, at] += folded(g)
            acc[1, :, at] += folded(g * zcm[l, rows, :])
        return carry

    lax.fori_loop(0, 4, middle, 0)
    own = jnp.concatenate(
        [
            jnp.sum(acc[0, :, :MID], axis=0, keepdims=True),
            jnp.sum(acc[1, :, :MID], axis=0, keepdims=True),
        ],
        axis=0,
    )
    finish2, drain2 = share(st2, own, s2s, s2r, "space")
    for slot, h in ((0, 0), (1, SLAB - 1)):
        for l in range(2):
            gsend[slot, :, l * 128 : l * 128 + 128] = gmid[
                l, pl.ds(h, PLANE, stride=SLAB), :
            ].astype(BF16)
    send_halos(gsend, ghalo, 1)

    def last(step, carry):
        cols = pl.ds(pl.multiple_of(step * 256, 256), 256)
        res = jnp.dot(rmt[...], ldz[:, cols], preferred_element_type=F32)
        pflat[0, pl.ds(step, MID, stride=4), :] = res[:, :128]
        pflat[1, pl.ds(step, MID, stride=4), :] = res[:, 128:]
        return carry

    lax.fori_loop(0, 4, last, 0)
    part[pl.ds(9 * MID, CH), :] = lanes(pflat, slice(None)).astype(BF16)

    core = lax.rem(me, 2)
    chip = lax.div(me, 2)
    partner = me + 1 - 2 * core

    def block(q, c):
        return pl.ds(pl.multiple_of((2 * q + c) * SHARE, SHARE), SHARE)

    def pair(q):
        return pltpu.make_async_remote_copy(
            src_ref=part.at[block(q, 1 - core)],
            dst_ref=ra.at[q],
            send_sem=as_.at[q],
            recv_sem=ar_.at[q],
            device_id=(partner, dp),
            device_id_type=MESH,
        )

    def chips(target, sender):
        return pltpu.make_async_remote_copy(
            src_ref=sb.at[target],
            dst_ref=rb.at[sender],
            send_sem=bs_.at[target],
            recv_sem=br_.at[sender],
            device_id=(2 * target + core, dp),
            device_id_type=MESH,
        )

    def start_pairs(lo, hi):
        def go(q, carry):
            pair(q).start()
            return carry

        lax.fori_loop(lo, hi, go, 0)

    def start_chips(lo, hi):
        def go(q, carry):
            pair(q).wait_recv()
            sb[q] = (part[block(q, core), :].astype(F32) + ra[q].astype(F32)).astype(BF16)

            @pl.when(q != chip)
            def _():
                chips(q, chip).start()

            return carry

        lax.fori_loop(lo, hi, go, 0)

    start_pairs(6, 8)

    sums2 = finish2()
    scale2, slope2, shift2, crossed2 = coefficients(sums2, MID, MID)
    std[dp, 0:1, MID : 2 * MID] = crossed2
    std[dp, 1:2, MID : 2 * MID] = sums2[0:1]

    for l in range(2):
        at = slice(l * 128, l * 128 + 128)
        stage[l, pl.ds(8, POS), :] = (
            (gmid[l] * scale2[:, at] + zcm[l] * slope2[:, at] + shift2[:, at])
            .astype(BF16)
            .astype(F32)
        )
    for h in range(SLAB):
        for l in range(2):
            for b in (-1, 0, 1):
                x = stage[l, pl.ds(8 + h - SLAB * b, PLANE, stride=SLAB), :]
                if b:
                    x = x * masks[(b + 1) // 2]
                lane = (b + 1) * MID + l * 128
                buf[pl.ds((h + 1) * PLANE, PLANE), lane : lane + 128] = x.astype(BF16)

    wait_halos(zsend, zhalo, 0)
    wait_halos(gsend, ghalo, 1)
    for side in range(2):
        present = me > 0 if side == 0 else me < NS - 1
        for l in range(2):
            at = slice(l * 128, l * 128 + 128)
            z = zhalo[side, :, at].astype(F32) - mean(MID + 128 * l, 128)
            dz = (
                (ghalo[side, :, at].astype(F32) * scale2[:, at] + z * slope2[:, at] + shift2[:, at])
                .astype(BF16)
                .astype(F32)
            )
            hstage[side, l, pl.ds(8, PLANE), :] = jnp.where(present, dz, 0.0)
            for b in (-1, 0, 1):
                x = hstage[side, l, pl.ds(8 - b, PLANE), :]
                if b:
                    x = x * masks[(b + 1) // 2]
                lane = (b + 1) * MID + l * 128
                buf[pl.ds(side * 5 * PLANE, PLANE), lane : lane + 128] = x.astype(BF16)

    def taps(step, carry):
        rows = pl.ds(pl.multiple_of((2 - step) * PLANE, PLANE), POS)
        for b in range(3):
            res = jnp.dot(
                rft[...], buf[rows, b * MID : b * MID + MID], preferred_element_type=F32
            )
            at = pl.ds(pl.multiple_of((3 * step + b) * MID, MID), MID)
            part[at, :] = res.astype(BF16)
        return carry

    lax.fori_loop(0, 3, taps, 0)
    start_pairs(0, 6)

    acc[...] = jnp.zeros_like(acc)
    mean3 = mean(0, MID)

    def conv(h, carry):
        total = jnp.zeros((PLANE, MID), F32)
        for a in range(3):
            rows = pl.ds(pl.multiple_of((h + 2 - a) * PLANE, PLANE), PLANE)
            total += lax.dot_general(buf[rows, :], wcat[a], NT, preferred_element_type=F32)
        rows = pl.ds(pl.multiple_of(h * PLANE, PLANE), PLANE)
        for l in range(2):
            at = slice(l * 128, l * 128 + 128)
            g = jnp.where(rfh[rows, at].astype(F32) > 0, total[:, at], 0.0)
            gfirst[l, pl.ds(h, PLANE, stride=SLAB), :] = g
            z = zfh[rows, at].astype(F32) - mean3[:, at]
            acc[0, :, at] += folded(g)
            acc[1, :, at] += folded(g * z)
        return carry

    lax.fori_loop(0, SLAB, conv, 0)
    own = jnp.concatenate(
        [
            jnp.sum(acc[0, :, :MID], axis=0, keepdims=True),
            jnp.sum(acc[1, :, :MID], axis=0, keepdims=True),
        ],
        axis=0,
    )
    finish3, drain3 = share(st3, own, s3s, s3r, "space")

    start_chips(0, 8)

    sums3 = finish3()
    scale3, slope3, shift3, crossed3 = coefficients(sums3, 0, MID)
    std[dp, 0:1, :MID] = crossed3
    std[dp, 1:2, :MID] = sums3[0:1]
    finish4, drain4 = share(std, std[dp], sds, sdr, "dp")

    for l in range(2):
        at = slice(l * 128, l * 128 + 128)
        z = pf[l].astype(F32) - mean3[:, at]
        ob[l] = (gfirst[l] * scale3[:, at] + z * slope3[:, at] + shift3[:, at]).astype(BF16)
    outs = [
        pltpu.make_async_copy(ob4.at[l], out_hbm.at[:, :, pl.ds(l * 128, 128)], osem.at[l])
        for l in range(2)
    ]
    for copy in outs:
        copy.start()

    tc[pl.ds(0, SHARE), :] = part[block(chip, core), :].astype(F32) + ra[chip].astype(F32)

    def gather(k, carry):
        sender = lax.rem(chip + k, 8)
        chips(sender, sender).wait_recv()
        tc[pl.ds(0, SHARE), :] += rb[sender].astype(F32)
        return carry

    lax.fori_loop(1, 8, gather, 0)
    tc[pl.ds(SHARE, 8), :] = jnp.zeros((8, 256), F32)
    for d in range(ND):
        sc[d] = tc[pl.ds(d * PIECE, 16), :].astype(BF16)
    rc[dp] = sc[dp]

    def shares(target, sender):
        return pltpu.make_async_remote_copy(
            src_ref=sc.at[target],
            dst_ref=rc.at[sender],
            send_sem=cs_.at[target],
            recv_sem=cr_.at[sender],
            device_id=(me, target),
            device_id_type=MESH,
        )

    def go(k, carry):
        shares(lax.rem(dp + k, ND), dp).start()
        return carry

    lax.fori_loop(1, ND, go, 0)

    ng_ref[...] = finish4() * FACTOR

    def wait(k, carry):
        other = lax.rem(dp + k, ND)
        shares(other, other).wait_recv()
        return carry

    lax.fori_loop(1, ND, wait, 0)
    mine = jnp.sum(rc[...].astype(F32), axis=0) * FACTOR
    for r in range(PIECE):
        wg_ref[2 * r : 2 * r + 1, :] = mine[r : r + 1, :128]
        wg_ref[2 * r + 1 : 2 * r + 2, :] = mine[r : r + 1, 128:]

    def drain_exchange(k, carry):
        exchange(lax.rem(me + k, NS), me).wait_send()
        return carry

    lax.fori_loop(1, NS, drain_exchange, 0)
    for drain in (drain1, drain2, drain3, drain4):
        drain()

    def drain_pairs(q, carry):
        pair(q).wait_send()

        @pl.when(q != chip)
        def _():
            chips(q, chip).wait_send()

        return carry

    lax.fori_loop(0, 8, drain_pairs, 0)

    def drain_shares(k, carry):
        shares(lax.rem(dp + k, ND), dp).wait_send()
        return carry

    lax.fori_loop(1, ND, drain_shares, 0)
    for copy in outs:
        copy.wait()


def shards(
    deep_grad, deep_weight, pre_first, relu_first, pre_middle, relu_middle, pre_last,
    block_output, weight_middle, weight_last, norm_mean, norm_rstd, norm_gain,
):
    def turned(x):
        return jnp.transpose(x, (0, 2, 1, 3)).reshape(PLANE, SLAB, x.shape[-1])

    any_spec = pl.BlockSpec(memory_space=pl.ANY)
    vmem_spec = pl.BlockSpec(memory_space=pltpu.VMEM)
    v = lambda shape, dtype: pltpu.VMEM(shape, dtype)
    dma = lambda *shape: pltpu.SemaphoreType.DMA(shape)
    scratch = [
        v((COLS, ROWS, MID4), BF16),
        v((NS, BLOCK, MID4), BF16),
        v((POS, MID4), BF16),
        v((CH, MID4), BF16),
        v((8, PLANE, SLAB, 128), BF16),
        v((8, PLANE, SLAB, 128), BF16),
        v((2, PLANE, SLAB, 128), BF16),
        v((2, PLANE, SLAB, 128), BF16),
        v((2, PLANE, SLAB, 128), BF16),
        v((2, PLANE, SLAB, 128), BF16),
        v((MID, CH), BF16),
        v((3, MID, 3 * MID), BF16),
        v((POS, CH), BF16),
        v((POS, CH), BF16),
        v((2, POS, 128), F32),
        v((2, POS, 128), F32),
        v((2, POS + 16, 128), F32),
        v((2, 2, PLANE + 16, 128), F32),
        v((6 * PLANE, 3 * MID), BF16),
        v((POS, MID), BF16),
        v((MID, POS), BF16),
        v((MID, POS), BF16),
        v((POS, MID), BF16),
        v((2, POS, 128), F32),
        v((2, PLANE, SLAB, 128), BF16),
        v((2, 8, CH), F32),
        v((NS, 2, CH), F32),
        v((NS, 2, MID), F32),
        v((NS, 2, MID), F32),
        v((ND, 2, CH + 2 * MID), F32),
        v((2, PLANE, MID), BF16),
        v((2, PLANE, MID), BF16),
        v((2, PLANE, MID), BF16),
        v((2, PLANE, MID), BF16),
        v((2, PLANE, 128), F32),
        v((2, CH, 128), F32),
        v((FLAT, 256), BF16),
        v((8, SHARE, 256), BF16),
        v((8, SHARE, 256), BF16),
        v((8, SHARE, 256), BF16),
        v((SHARE + 8, 256), F32),
        v((ND, 16, 256), BF16),
        v((ND, 16, 256), BF16),
        dma(36), dma(4), dma(2),
        dma(16), dma(16),
        dma(16), dma(16), dma(16), dma(16), dma(16), dma(16), dma(16), dma(16),
        dma(2, 2), dma(2, 2),
        dma(8), dma(8), dma(8), dma(8), dma(16), dma(16),
    ]
    first, weights, norms = pl.pallas_call(
        kernel,
        out_shape=(
            jax.ShapeDtypeStruct((PLANE, SLAB, MID), BF16),
            jax.ShapeDtypeStruct((2 * PIECE, 128), F32),
            jax.ShapeDtypeStruct((2, CH + 2 * MID), F32),
        ),
        in_specs=[any_spec] * 10 + [vmem_spec] * 3,
        out_specs=(any_spec, vmem_spec, vmem_spec),
        scratch_shapes=scratch,
        compiler_params=pltpu.CompilerParams(
            collective_id=0, has_side_effects=True, vmem_limit_bytes=60 << 20
        ),
    )(
        jnp.transpose(deep_grad, (0, 2, 1, 3)).reshape(COLS, ROWS, MID4),
        deep_weight,
        turned(pre_first),
        turned(relu_first),
        turned(pre_middle),
        turned(relu_middle),
        turned(pre_last),
        turned(block_output),
        weight_middle,
        weight_last,
        norm_mean,
        norm_rstd,
        norm_gain,
    )
    first = jnp.transpose(first.reshape(GROUP, COLS, SLAB, MID), (0, 2, 1, 3))
    return first, weights.reshape(-1), norms


def solution(mesh):
    return jax.shard_map(
        shards,
        mesh=mesh,
        in_specs=(
            P(("dp", "space"), None, None, None),
            P(),
            P("dp", "space", None, None),
            P("dp", "space", None, None),
            P("dp", "space", None, None),
            P("dp", "space", None, None),
            P("dp", "space", None, None),
            P("dp", "space", None, None),
            P(),
            P(),
            P(),
            P(),
            P(),
        ),
        out_specs=(P("dp", "space", None, None), P(("space", "dp")), P()),
        check_vma=False,
    )
```

```python
import functools
import math

import jax
import jax.numpy as jnp
from jax import lax
from jax.experimental import pallas as pl
from jax.experimental.pallas import tpu as pltpu
from jax.sharding import PartitionSpec as P

MESH = pl.DeviceIdType.MESH
F32 = jnp.float32
BF16 = jnp.bfloat16

NS = 16
ND = 16
GROUP = 16
SLAB = 4
COLS = 20
ROWS = 64
CH = 1024
MID = 256
MID4 = 512
POS = GROUP * SLAB * COLS
PLANE = GROUP * COLS
BLOCK = SLAB * COLS
FLAT = 9 * MID + CH
SHARE = FLAT // NS
PIECE = SHARE // ND
M = float(GROUP * ROWS * COLS)
FACTOR = 1.0 / math.sqrt(M * ND)
NT = (((1,), (1,)), ((), ()))
ORDER = (12, 4, 13, 5, 11, 3, 10, 6, 14, 2, 9, 7, 15, 8, 1)


def folded(values):
    return jnp.sum(values.reshape(-1, 8, values.shape[-1]), axis=0)


def lanes(ref, rows):
    return jnp.concatenate([ref[0, rows, :], ref[1, rows, :]], axis=1)


def kernel(
    dg_hbm, wd_hbm, pf_hbm, rf_hbm, pm_hbm, rm_hbm, pz_hbm, bo_hbm, wm_hbm, wl_hbm,
    mean_ref, rstd_ref, gain_ref,
    out_hbm, wg_ref, ng_ref,
    dgv, send, recv, wd, bo4, pz4, pf4, rf4, pm4, rm4, wl, wcat,
    glast, ldz, zcm, gmid, stage, hstage, buf, rfh, rft, rmt, zfh, gfirst, ob4,
    acc, st1, st2, st3, std,
    zsend, gsend, zhalo, ghalo, masks,
    pflat, part, ra, sb, rb, tc, sc, rc,
    lsem, dsem, osem,
    a2a_s, a2a_r, s1s, s1r, s2s, s2r, s3s, s3r, sds, sdr, hs, hr,
    as_, ar_, bs_, br_, cs_, cr_,
    near, wide, other,
):
    me = lax.axis_index("space")
    dp = lax.axis_index("dp")

    dg_copies = [
        pltpu.make_async_copy(
            dg_hbm.at[:, pl.ds(16 * u, 16), :], dgv.at[:, pl.ds(16 * u, 16), :], dsem.at[u]
        )
        for u in range(4)
    ]
    for copy in dg_copies:
        copy.start()
    loads = []

    def load(src, dst):
        copy = pltpu.make_async_copy(src, dst, lsem.at[len(loads)])
        copy.start()
        loads.append(copy)
        return copy

    def load_tiles(src, dst, count):
        return [load(src.at[:, :, pl.ds(128 * j, 128)], dst.at[j]) for j in range(count)]

    barrier = pltpu.get_barrier_semaphore()

    half, z = lax.div(dp, 8), lax.rem(dp, 8)

    def along(k):
        return (me, half * 8 + lax.rem(z + k, 8))

    across = (me, lax.rem(dp + 8, ND))

    def signal(sem, device):
        pl.semaphore_signal(sem, inc=1, device_id=device, device_id_type=MESH)

    for k in ORDER:
        signal(barrier, (lax.rem(me + k, NS), dp))
    signal(barrier, along(1))
    signal(barrier, along(7))
    signal(barrier, across)

    ld_pm = load_tiles(pm_hbm, pm4, 2)
    ld_rm = load_tiles(rm_hbm, rm4, 2)
    ld_wd = [load(wd_hbm, wd)]
    ld_bo = load_tiles(bo_hbm, bo4, 8)
    ld_pz = load_tiles(pz_hbm, pz4, 8)
    ld_rf = load_tiles(rf_hbm, rf4, 2)
    ld_pf = load_tiles(pf_hbm, pf4, 2)
    ld_wl = [load(wl_hbm, wl)]
    ld_wc = [
        load(wm_hbm.at[pl.ds(t * MID, MID)], wcat.at[t // 3, :, pl.ds((t % 3) * MID, MID)])
        for t in range(9)
    ]

    bo = bo4.reshape(8, POS, 128)
    pz = pz4.reshape(8, POS, 128)
    pf = pf4.reshape(2, POS, 128)
    rf = rf4.reshape(2, POS, 128)
    pm = pm4.reshape(2, POS, 128)
    rm = rm4.reshape(2, POS, 128)
    ob = ob4.reshape(2, POS, 128)

    def exchange(target, sender):
        return pltpu.make_async_remote_copy(
            src_ref=send.at[target],
            dst_ref=recv.at[pl.ds(pl.multiple_of(sender * BLOCK, BLOCK), BLOCK)],
            send_sem=a2a_s.at[target],
            recv_sem=a2a_r.at[sender],
            device_id=(target, dp),
            device_id_type=MESH,
        )

    my_group = lax.div(me, 4)
    low = lax.broadcasted_iota(jnp.int32, (10, 8, MID4), 1) < 4
    for u in range(4):
        dg_copies[u].wait()
        x = dgv[:, 16 * u : 16 * u + 16, :].astype(F32)
        for part_ in range(2):
            y = x[:, 8 * part_ : 8 * part_ + 8, :].reshape(10, 2, 8, MID4)
            even, odd = y[:, 0], y[:, 1]
            first = jnp.where(low, even, pltpu.roll(odd, 4, 1))
            second = jnp.where(low, pltpu.roll(even, 4, 1), odd)
            send[u * 4 + 2 * part_] = first.reshape(BLOCK, MID4).astype(BF16)
            send[u * 4 + 2 * part_ + 1] = second.reshape(BLOCK, MID4).astype(BF16)
    pl.semaphore_wait(barrier, NS + 2)
    for k in ORDER:
        exchange(lax.rem(me + k, NS), me).start()
    signal(near, along(1))
    signal(near, along(7))
    recv[pl.ds(pl.multiple_of(me * BLOCK, BLOCK), BLOCK), :] = send[me]

    mean = lambda lo, n: mean_ref[pl.ds(lo, n)].reshape(1, n)
    rstd = lambda lo, n: rstd_ref[pl.ds(lo, n)].reshape(1, n)
    gain = lambda lo, n: gain_ref[pl.ds(lo, n)].reshape(1, n)

    def halo(src, dst, sem, to_up):
        slot = 0 if to_up else 1
        target = lax.rem(me + (NS - 1 if to_up else 1), NS)
        return pltpu.make_async_remote_copy(
            src_ref=src.at[slot],
            dst_ref=dst.at[1 - slot],
            send_sem=hs.at[sem, slot],
            recv_sem=hr.at[sem, 1 - slot],
            device_id=(target, dp),
            device_id_type=MESH,
        )

    def send_halos(src, dst, sem):
        @pl.when(me > 0)
        def _():
            halo(src, dst, sem, True).start()

        @pl.when(me < NS - 1)
        def _():
            halo(src, dst, sem, False).start()

    def wait_halos(src, dst, sem):
        @pl.when(me > 0)
        def _():
            halo(src, dst, sem, True).wait_send()
            halo(src, dst, sem, False).wait_recv()

        @pl.when(me < NS - 1)
        def _():
            halo(src, dst, sem, False).wait_send()
            halo(src, dst, sem, True).wait_recv()

    for copy in ld_pm:
        copy.wait()
    for l in range(2):
        raw = pm[l].astype(F32)
        stage[l, pl.ds(8, POS), :] = raw
        zcm[l] = raw - mean(MID + 128 * l, 128)
    for slot, h in ((0, 0), (1, SLAB - 1)):
        for l in range(2):
            zsend[slot, :, l * 128 : l * 128 + 128] = stage[
                l, pl.ds(8 + h, PLANE, stride=SLAB), :
            ].astype(BF16)

    for copy in ld_rm:
        copy.wait()
    for l in range(2):
        rmt[pl.ds(l * 128, 128), :] = rm[l].T

    row = lax.broadcasted_iota(jnp.int32, (PLANE, 128), 0)
    column = lax.rem(row, COLS)
    masks[0] = jnp.where(column == COLS - 1, 0.0, 1.0)
    masks[1] = jnp.where(column == 0, 0.0, 1.0)

    for copy in ld_rf:
        copy.wait()
    for l in range(2):
        stage[l, pl.ds(8, POS), :] = rf[l].astype(F32)
    for h in range(SLAB):
        for l in range(2):
            rfh[pl.ds(h * PLANE, PLANE), l * 128 : l * 128 + 128] = stage[
                l, pl.ds(8 + h, PLANE, stride=SLAB), :
            ].astype(BF16)
    for l in range(2):
        rft[pl.ds(l * 128, 128), :] = rfh[:, l * 128 : l * 128 + 128].T

    for copy in ld_pf:
        copy.wait()
    for l in range(2):
        stage[l, pl.ds(8, POS), :] = pf[l].astype(F32)
    for h in range(SLAB):
        for l in range(2):
            zfh[pl.ds(h * PLANE, PLANE), l * 128 : l * 128 + 128] = stage[
                l, pl.ds(8 + h, PLANE, stride=SLAB), :
            ].astype(BF16)
    for l in range(2):
        stage[l, pl.ds(0, 8), :] = jnp.zeros((8, 128), F32)
        stage[l, pl.ds(8 + POS, 8), :] = jnp.zeros((8, 128), F32)
        for side in range(2):
            hstage[side, l, pl.ds(0, 8), :] = jnp.zeros((8, 128), F32)
            hstage[side, l, pl.ds(8 + PLANE, 8), :] = jnp.zeros((8, 128), F32)

    for copy in ld_wd + ld_bo + ld_pz + ld_wl + ld_wc:
        copy.wait()
    pl.semaphore_wait(near, 2)
    signal(wide, along(2))
    signal(wide, along(6))

    acc[...] = jnp.zeros_like(acc)

    def project(step, carry):
        group = lax.rem(my_group + jnp.where(step == 0, 0, jnp.where(step == 1, 2, jnp.where(step == 2, 3, 1))), 4)
        for q in range(4):
            sender = group * 4 + q

            @pl.when(sender != me)
            def _():
                exchange(sender, sender).wait_recv()

        rows = pl.ds(pl.multiple_of(group * PLANE, PLANE), PLANE)
        for c in range(4):
            up = lax.dot_general(
                recv[rows, :], wd[pl.ds(c * 256, 256), :], NT, preferred_element_type=F32
            )
            for l in range(2):
                j = 2 * c + l
                at = slice(j * 128, j * 128 + 128)
                g = up[:, l * 128 : l * 128 + 128].astype(BF16).astype(F32)
                g = jnp.where(bo[j, rows, :].astype(F32) > 0, g, 0.0)
                glast[rows, at] = g.astype(BF16)
                z = pz[j, rows, :].astype(F32) - mean(2 * MID + 128 * j, 128)
                acc[0, :, at] += folded(g)
                acc[1, :, at] += folded(g * z)
        return carry

    lax.fori_loop(0, 4, project, 0)

    def share(slots, own, sends, recvs, axis):
        at = me if axis == "space" else dp

        def desc(other, sender):
            return pltpu.make_async_remote_copy(
                src_ref=slots.at[at],
                dst_ref=slots.at[sender],
                send_sem=sends.at[other],
                recv_sem=recvs.at[sender],
                device_id=(other, dp) if axis == "space" else (me, other),
                device_id_type=MESH,
            )

        slots[at] = own

        for k in ORDER:
            desc(lax.rem(at + k, 16), at).start()

        def finish():
            def wait(k, carry):
                other = lax.rem(at + k, 16)
                desc(other, other).wait_recv()
                return carry

            lax.fori_loop(1, 16, wait, 0)
            return jnp.sum(slots[...], axis=0)

        def drain():
            def wait(k, carry):
                desc(lax.rem(at + k, 16), at).wait_send()
                return carry

            lax.fori_loop(1, 16, wait, 0)

        return finish, drain

    def coefficients(sums, lo, n):
        scale = gain(lo, n) * rstd(lo, n)
        crossed = sums[1:2] * rstd(lo, n)
        slope = -scale * rstd(lo, n) * crossed * (1.0 / M)
        shift = -scale * sums[0:1] * (1.0 / M)
        return scale, slope, shift, crossed

    own = jnp.concatenate(
        [jnp.sum(acc[0], axis=0, keepdims=True), jnp.sum(acc[1], axis=0, keepdims=True)], axis=0
    )
    finish1, drain1 = share(st1, own, s1s, s1r, "space")
    send_halos(zsend, zhalo, 0)
    pl.semaphore_wait(wide, 2)
    signal(other, across)

    def drain_exchange(k, carry):
        exchange(lax.rem(me + k, NS), me).wait_send()
        return carry

    lax.fori_loop(1, NS, drain_exchange, 0)
    sums1 = finish1()
    scale1, slope1, shift1, crossed1 = coefficients(sums1, 2 * MID, CH)
    std[dp, 0:1, 2 * MID :] = crossed1
    std[dp, 1:2, 2 * MID :] = sums1[0:1]

    acc[...] = jnp.zeros_like(acc)
    mean1 = mean(2 * MID, CH)

    def middle(step, carry):
        rows = pl.ds(step * PLANE, PLANE)
        for j in range(8):
            at = slice(j * 128, j * 128 + 128)
            z = pz[j, rows, :].astype(F32) - mean1[:, at]
            ldz[rows, at] = (
                glast[rows, at].astype(F32) * scale1[:, at] + z * slope1[:, at] + shift1[:, at]
            ).astype(BF16)
        mi = lax.dot_general(ldz[rows, :], wl[...], NT, preferred_element_type=F32)
        for l in range(2):
            at = slice(l * 128, l * 128 + 128)
            g = jnp.where(rm[l, rows, :].astype(F32) > 0, mi[:, at], 0.0)
            gmid[l, rows, :] = g
            acc[0, :, at] += folded(g)
            acc[1, :, at] += folded(g * zcm[l, rows, :])
        return carry

    for step in range(4):
        middle(step, 0)
    own = jnp.concatenate(
        [
            jnp.sum(acc[0, :, :MID], axis=0, keepdims=True),
            jnp.sum(acc[1, :, :MID], axis=0, keepdims=True),
        ],
        axis=0,
    )
    finish2, drain2 = share(st2, own, s2s, s2r, "space")
    for slot, h in ((0, 0), (1, SLAB - 1)):
        for l in range(2):
            gsend[slot, :, l * 128 : l * 128 + 128] = gmid[
                l, pl.ds(h, PLANE, stride=SLAB), :
            ].astype(BF16)
    send_halos(gsend, ghalo, 1)
    drain1()

    def last(step, carry):
        cols = pl.ds(step * 256, 256)
        res = jnp.dot(rmt[...], ldz[:, cols], preferred_element_type=F32)
        pflat[0, pl.ds(step, MID, stride=4), :] = res[:, :128]
        pflat[1, pl.ds(step, MID, stride=4), :] = res[:, 128:]
        return carry

    for step in range(4):
        last(step, 0)
    part[pl.ds(9 * MID, CH), :] = lanes(pflat, slice(None)).astype(BF16)

    core = lax.rem(me, 2)
    chip = lax.div(me, 2)
    partner = me + 1 - 2 * core

    def block(q, c):
        return pl.ds(pl.multiple_of((2 * q + c) * SHARE, SHARE), SHARE)

    def pair(q):
        return pltpu.make_async_remote_copy(
            src_ref=part.at[block(q, 1 - core)],
            dst_ref=ra.at[q],
            send_sem=as_.at[q],
            recv_sem=ar_.at[q],
            device_id=(partner, dp),
            device_id_type=MESH,
        )

    def chips(target, sender):
        return pltpu.make_async_remote_copy(
            src_ref=sb.at[target],
            dst_ref=rb.at[sender],
            send_sem=bs_.at[target],
            recv_sem=br_.at[sender],
            device_id=(2 * target + core, dp),
            device_id_type=MESH,
        )

    def start_pairs(lo, hi):
        def go(q, carry):
            pair(q).start()
            return carry

        lax.fori_loop(lo, hi, go, 0)

    def start_chips(lo, hi):
        def go(q, carry):
            pair(q).wait_recv()
            sb[q] = (part[block(q, core), :].astype(F32) + ra[q].astype(F32)).astype(BF16)

            @pl.when(q != chip)
            def _():
                chips(q, chip).start()

            return carry

        lax.fori_loop(lo, hi, go, 0)

    start_pairs(6, 8)

    sums2 = finish2()
    scale2, slope2, shift2, crossed2 = coefficients(sums2, MID, MID)
    std[dp, 0:1, MID : 2 * MID] = crossed2
    std[dp, 1:2, MID : 2 * MID] = sums2[0:1]

    for l in range(2):
        at = slice(l * 128, l * 128 + 128)
        stage[l, pl.ds(8, POS), :] = (
            (gmid[l] * scale2[:, at] + zcm[l] * slope2[:, at] + shift2[:, at])
            .astype(BF16)
            .astype(F32)
        )
    for h in range(SLAB):
        for l in range(2):
            for b in (-1, 0, 1):
                x = stage[l, pl.ds(8 + h - SLAB * b, PLANE, stride=SLAB), :]
                if b:
                    x = x * masks[(b + 1) // 2]
                lane = (b + 1) * MID + l * 128
                buf[pl.ds((h + 1) * PLANE, PLANE), lane : lane + 128] = x.astype(BF16)

    wait_halos(zsend, zhalo, 0)
    wait_halos(gsend, ghalo, 1)
    for side in range(2):
        present = me > 0 if side == 0 else me < NS - 1
        for l in range(2):
            at = slice(l * 128, l * 128 + 128)
            z = zhalo[side, :, at].astype(F32) - mean(MID + 128 * l, 128)
            dz = (
                (ghalo[side, :, at].astype(F32) * scale2[:, at] + z * slope2[:, at] + shift2[:, at])
                .astype(BF16)
                .astype(F32)
            )
            hstage[side, l, pl.ds(8, PLANE), :] = jnp.where(present, dz, 0.0)
            for b in (-1, 0, 1):
                x = hstage[side, l, pl.ds(8 - b, PLANE), :]
                if b:
                    x = x * masks[(b + 1) // 2]
                lane = (b + 1) * MID + l * 128
                buf[pl.ds(side * 5 * PLANE, PLANE), lane : lane + 128] = x.astype(BF16)

    drain2()
    start_chips(6, 8)

    def taps(a):
        rows = pl.ds((2 - a) * PLANE, POS)
        for b in range(3):
            part[pl.ds((3 * a + b) * MID, MID), :] = jnp.dot(
                rft[...], buf[rows, b * MID : b * MID + MID], preferred_element_type=F32
            ).astype(BF16)

    taps(0)
    start_pairs(0, 1)
    taps(1)
    start_pairs(1, 3)
    start_chips(0, 1)
    taps(2)
    start_pairs(3, 6)
    start_chips(1, 3)

    acc[...] = jnp.zeros_like(acc)
    mean3 = mean(0, MID)

    def conv(h, carry):
        total = jnp.zeros((PLANE, MID), F32)
        for a in range(3):
            rows = pl.ds((h + 2 - a) * PLANE, PLANE)
            total += lax.dot_general(buf[rows, :], wcat[a], NT, preferred_element_type=F32)
        rows = pl.ds(h * PLANE, PLANE)
        for l in range(2):
            at = slice(l * 128, l * 128 + 128)
            g = jnp.where(rfh[rows, at].astype(F32) > 0, total[:, at], 0.0)
            gfirst[l, pl.ds(h, PLANE, stride=SLAB), :] = g
            z = zfh[rows, at].astype(F32) - mean3[:, at]
            acc[0, :, at] += folded(g)
            acc[1, :, at] += folded(g * z)
        return carry

    for h in range(SLAB):
        conv(h, 0)
        if h == 1:
            start_chips(3, 6)
    own = jnp.concatenate(
        [
            jnp.sum(acc[0, :, :MID], axis=0, keepdims=True),
            jnp.sum(acc[1, :, :MID], axis=0, keepdims=True),
        ],
        axis=0,
    )
    finish3, drain3 = share(st3, own, s3s, s3r, "space")

    sums3 = finish3()
    scale3, slope3, shift3, crossed3 = coefficients(sums3, 0, MID)
    std[dp, 0:1, :MID] = crossed3
    std[dp, 1:2, :MID] = sums3[0:1]
    pl.semaphore_wait(other, 1)
    finish4, drain4 = share(std, std[dp], sds, sdr, "dp")
    drain3()

    for l in range(2):
        at = slice(l * 128, l * 128 + 128)
        z = pf[l].astype(F32) - mean3[:, at]
        ob[l] = (gfirst[l] * scale3[:, at] + z * slope3[:, at] + shift3[:, at]).astype(BF16)
    outs = [
        pltpu.make_async_copy(ob4.at[l], out_hbm.at[:, :, pl.ds(l * 128, 128)], osem.at[l])
        for l in range(2)
    ]
    for copy in outs:
        copy.start()

    tc[pl.ds(0, SHARE), :] = part[block(chip, core), :].astype(F32) + ra[chip].astype(F32)

    def gather(k, carry):
        sender = lax.rem(chip + k, 8)
        chips(sender, sender).wait_recv()
        tc[pl.ds(0, SHARE), :] += rb[sender].astype(F32)
        return carry

    lax.fori_loop(1, 8, gather, 0)
    tc[pl.ds(SHARE, 8), :] = jnp.zeros((8, 256), F32)
    for d in range(ND):
        sc[d] = tc[pl.ds(d * PIECE, 16), :].astype(BF16)
    rc[dp] = sc[dp]

    def shares(target, sender):
        return pltpu.make_async_remote_copy(
            src_ref=sc.at[target],
            dst_ref=rc.at[sender],
            send_sem=cs_.at[target],
            recv_sem=cr_.at[sender],
            device_id=(me, target),
            device_id_type=MESH,
        )

    for k in ORDER:
        shares(lax.rem(dp + k, ND), dp).start()

    def drain_pairs(q, carry):
        pair(q).wait_send()

        @pl.when(q != chip)
        def _():
            chips(q, chip).wait_send()

        return carry

    lax.fori_loop(0, 8, drain_pairs, 0)

    ng_ref[...] = finish4() * FACTOR

    def wait(k, carry):
        other = lax.rem(dp + k, ND)
        shares(other, other).wait_recv()
        return carry

    lax.fori_loop(1, ND, wait, 0)
    mine = jnp.sum(rc[...].astype(F32), axis=0) * FACTOR
    for r in range(PIECE):
        wg_ref[2 * r : 2 * r + 1, :] = mine[r : r + 1, :128]
        wg_ref[2 * r + 1 : 2 * r + 2, :] = mine[r : r + 1, 128:]

    drain4()

    def drain_shares(k, carry):
        shares(lax.rem(dp + k, ND), dp).wait_send()
        return carry

    lax.fori_loop(1, ND, drain_shares, 0)
    for copy in outs:
        copy.wait()


def settle(a, b, c, x, y, z, sem):
    copies = [
        pltpu.make_async_copy(src, dst, sem.at[i]) for i, (src, dst) in enumerate(((a, x), (b, y), (c, z)))
    ]
    for copy in copies:
        copy.start()
    for copy in copies:
        copy.wait()


def shards(
    deep_grad, deep_weight, pre_first, relu_first, pre_middle, relu_middle, pre_last,
    block_output, weight_middle, weight_last, norm_mean, norm_rstd, norm_gain,
):
    def turned(x):
        return jnp.transpose(x, (0, 2, 1, 3)).reshape(PLANE, SLAB, x.shape[-1])

    any_spec = pl.BlockSpec(memory_space=pl.ANY)
    vmem_spec = pl.BlockSpec(memory_space=pltpu.VMEM)
    v = lambda shape, dtype: pltpu.VMEM(shape, dtype)
    dma = lambda *shape: pltpu.SemaphoreType.DMA(shape)
    scratch = [
        v((COLS, ROWS, MID4), BF16),
        v((NS, BLOCK, MID4), BF16),
        v((POS, MID4), BF16),
        v((CH, MID4), BF16),
        v((8, PLANE, SLAB, 128), BF16),
        v((8, PLANE, SLAB, 128), BF16),
        v((2, PLANE, SLAB, 128), BF16),
        v((2, PLANE, SLAB, 128), BF16),
        v((2, PLANE, SLAB, 128), BF16),
        v((2, PLANE, SLAB, 128), BF16),
        v((MID, CH), BF16),
        v((3, MID, 3 * MID), BF16),
        v((POS, CH), BF16),
        v((POS, CH), BF16),
        v((2, POS, 128), F32),
        v((2, POS, 128), F32),
        v((2, POS + 16, 128), F32),
        v((2, 2, PLANE + 16, 128), F32),
        v((6 * PLANE, 3 * MID), BF16),
        v((POS, MID), BF16),
        v((MID, POS), BF16),
        v((MID, POS), BF16),
        v((POS, MID), BF16),
        v((2, POS, 128), F32),
        v((2, PLANE, SLAB, 128), BF16),
        v((2, 8, CH), F32),
        v((NS, 2, CH), F32),
        v((NS, 2, MID), F32),
        v((NS, 2, MID), F32),
        v((ND, 2, CH + 2 * MID), F32),
        v((2, PLANE, MID), BF16),
        v((2, PLANE, MID), BF16),
        v((2, PLANE, MID), BF16),
        v((2, PLANE, MID), BF16),
        v((2, PLANE, 128), F32),
        v((2, CH, 128), F32),
        v((FLAT, 256), BF16),
        v((8, SHARE, 256), BF16),
        v((8, SHARE, 256), BF16),
        v((8, SHARE, 256), BF16),
        v((SHARE + 8, 256), F32),
        v((ND, 16, 256), BF16),
        v((ND, 16, 256), BF16),
        dma(36), dma(4), dma(2),
        dma(16), dma(16),
        dma(16), dma(16), dma(16), dma(16), dma(16), dma(16), dma(16), dma(16),
        dma(2, 2), dma(2, 2),
        dma(8), dma(8), dma(8), dma(8), dma(16), dma(16),
        pltpu.SemaphoreType.REGULAR, pltpu.SemaphoreType.REGULAR, pltpu.SemaphoreType.REGULAR,
    ]
    first, weights, norms = pl.pallas_call(
        kernel,
        out_shape=(
            jax.ShapeDtypeStruct((PLANE, SLAB, MID), BF16),
            jax.ShapeDtypeStruct((2 * PIECE, 128), F32),
            jax.ShapeDtypeStruct((2, CH + 2 * MID), F32),
        ),
        in_specs=[any_spec] * 10 + [vmem_spec] * 3,
        out_specs=(any_spec, vmem_spec, vmem_spec),
        scratch_shapes=scratch,
        compiler_params=pltpu.CompilerParams(
            collective_id=0, has_side_effects=True, vmem_limit_bytes=60 << 20
        ),
    )(
        jnp.transpose(deep_grad, (0, 2, 1, 3)).reshape(COLS, ROWS, MID4),
        deep_weight,
        turned(pre_first),
        turned(relu_first),
        turned(pre_middle),
        turned(relu_middle),
        turned(pre_last),
        turned(block_output),
        weight_middle,
        weight_last,
        norm_mean,
        norm_rstd,
        norm_gain,
    )
    first, weights, norms = pl.pallas_call(
        settle,
        out_shape=tuple(jax.ShapeDtypeStruct(x.shape, x.dtype) for x in (first, weights, norms)),
        in_specs=[any_spec] * 3,
        out_specs=(any_spec,) * 3,
        scratch_shapes=[dma(3)],
        compiler_params=pltpu.CompilerParams(vmem_limit_bytes=60 << 20),
    )(first, weights, norms)
    first = jnp.transpose(first.reshape(GROUP, COLS, SLAB, MID), (0, 2, 1, 3))
    return first, weights.reshape(-1), norms


def solution(mesh):
    return jax.shard_map(
        shards,
        mesh=mesh,
        in_specs=(
            P(("dp", "space"), None, None, None),
            P(),
            P("dp", "space", None, None),
            P("dp", "space", None, None),
            P("dp", "space", None, None),
            P("dp", "space", None, None),
            P("dp", "space", None, None),
            P("dp", "space", None, None),
            P(),
            P(),
            P(),
            P(),
            P(),
        ),
        out_specs=(P("dp", "space", None, None), P(("space", "dp")), P()),
        check_vma=False,
    )
```

```python
import functools
import math

import jax
import jax.numpy as jnp
from jax import lax
from jax.experimental import pallas as pl
from jax.experimental.pallas import tpu as pltpu
from jax.sharding import PartitionSpec as P

MESH = pl.DeviceIdType.MESH
F32 = jnp.float32
BF16 = jnp.bfloat16

NS = 16
ND = 16
GROUP = 16
SLAB = 4
COLS = 20
ROWS = 64
CH = 1024
MID = 256
MID4 = 512
POS = GROUP * SLAB * COLS
PLANE = GROUP * COLS
BLOCK = SLAB * COLS
FLAT = 9 * MID + CH
SHARE = FLAT // NS
PIECE = SHARE // ND
M = float(GROUP * ROWS * COLS)
FACTOR = 1.0 / math.sqrt(M * ND)
NT = (((1,), (1,)), ((), ()))
ORDER = (12, 4, 13, 5, 11, 3, 10, 6, 14, 2, 9, 7, 15, 8, 1)


def folded(values):
    return jnp.sum(values.reshape(-1, 8, values.shape[-1]), axis=0)


def lanes(ref, rows):
    return jnp.concatenate([ref[0, rows, :], ref[1, rows, :]], axis=1)


def kernel(
    dg_hbm, wd_hbm, pf_hbm, rf_hbm, pm_hbm, rm_hbm, pz_hbm, bo_hbm, wm_hbm, wl_hbm,
    mean_ref, rstd_ref, gain_ref,
    out_hbm, wg_ref, ng_ref,
    dgv, send, recv, wd, bo4, pz4, pf4, rf4, pm4, rm4, wl, wcat,
    glast, ldz, zcm, gmid, stage, hstage, buf, rfh, rft, rmt, zfh, gfirst, ob4,
    acc, st1, st2, st3, st4, std,
    zsend, gsend, zhalo, ghalo, masks,
    pflat, part, ra, sb, rb, tc, sc, rc,
    lsem, dsem, osem,
    a2a_s, a2a_r, s1s, s1r, s2s, s2r, s3s, s3r, sds, sdr, hs, hr,
    as_, ar_, bs_, br_, cs_, cr_,
    near, wide, other,
):
    me = lax.axis_index("space")
    dp = lax.axis_index("dp")

    dg_copies = [
        pltpu.make_async_copy(
            dg_hbm.at[:, pl.ds(16 * u, 16), :], dgv.at[:, pl.ds(16 * u, 16), :], dsem.at[u]
        )
        for u in range(4)
    ]
    for copy in dg_copies:
        copy.start()
    loads = []

    def load(src, dst):
        copy = pltpu.make_async_copy(src, dst, lsem.at[len(loads)])
        copy.start()
        loads.append(copy)
        return copy

    def load_tiles(src, dst, count):
        return [load(src.at[:, :, pl.ds(128 * j, 128)], dst.at[j]) for j in range(count)]

    barrier = pltpu.get_barrier_semaphore()

    half, z = lax.div(dp, 8), lax.rem(dp, 8)

    def along(k):
        return (me, half * 8 + lax.rem(z + k, 8))

    across = (me, lax.rem(dp + 8, ND))

    def signal(sem, device):
        pl.semaphore_signal(sem, inc=1, device_id=device, device_id_type=MESH)

    for k in ORDER:
        signal(barrier, (lax.rem(me + k, NS), dp))
    signal(barrier, along(1))
    signal(barrier, along(7))
    signal(barrier, across)

    ld_pm = load_tiles(pm_hbm, pm4, 2)
    ld_rm = load_tiles(rm_hbm, rm4, 2)
    ld_wd = [load(wd_hbm, wd)]
    ld_bo = load_tiles(bo_hbm, bo4, 8)
    ld_pz = load_tiles(pz_hbm, pz4, 8)
    ld_rf = load_tiles(rf_hbm, rf4, 2)
    ld_pf = load_tiles(pf_hbm, pf4, 2)
    ld_wl = [load(wl_hbm, wl)]
    ld_wc = [
        load(wm_hbm.at[pl.ds(t * MID, MID)], wcat.at[t // 3, :, pl.ds((t % 3) * MID, MID)])
        for t in range(9)
    ]

    bo = bo4.reshape(8, POS, 128)
    pz = pz4.reshape(8, POS, 128)
    pf = pf4.reshape(2, POS, 128)
    rf = rf4.reshape(2, POS, 128)
    pm = pm4.reshape(2, POS, 128)
    rm = rm4.reshape(2, POS, 128)
    ob = ob4.reshape(2, POS, 128)

    def exchange(target, sender):
        return pltpu.make_async_remote_copy(
            src_ref=send.at[target],
            dst_ref=recv.at[pl.ds(pl.multiple_of(sender * BLOCK, BLOCK), BLOCK)],
            send_sem=a2a_s.at[target],
            recv_sem=a2a_r.at[sender],
            device_id=(target, dp),
            device_id_type=MESH,
        )

    my_group = lax.div(me, 4)
    low = lax.broadcasted_iota(jnp.int32, (10, 8, MID4), 1) < 4
    for u in range(4):
        dg_copies[u].wait()
        x = dgv[:, 16 * u : 16 * u + 16, :].astype(F32)
        for part_ in range(2):
            y = x[:, 8 * part_ : 8 * part_ + 8, :].reshape(10, 2, 8, MID4)
            even, odd = y[:, 0], y[:, 1]
            first = jnp.where(low, even, pltpu.roll(odd, 4, 1))
            second = jnp.where(low, pltpu.roll(even, 4, 1), odd)
            send[u * 4 + 2 * part_] = first.reshape(BLOCK, MID4).astype(BF16)
            send[u * 4 + 2 * part_ + 1] = second.reshape(BLOCK, MID4).astype(BF16)
    pl.semaphore_wait(barrier, NS + 2)
    for k in ORDER:
        exchange(lax.rem(me + k, NS), me).start()
    signal(near, along(1))
    signal(near, along(7))
    recv[pl.ds(pl.multiple_of(me * BLOCK, BLOCK), BLOCK), :] = send[me]

    mean = lambda lo, n: mean_ref[pl.ds(lo, n)].reshape(1, n)
    rstd = lambda lo, n: rstd_ref[pl.ds(lo, n)].reshape(1, n)
    gain = lambda lo, n: gain_ref[pl.ds(lo, n)].reshape(1, n)

    def halo(src, dst, sem, to_up):
        slot = 0 if to_up else 1
        target = lax.rem(me + (NS - 1 if to_up else 1), NS)
        return pltpu.make_async_remote_copy(
            src_ref=src.at[slot],
            dst_ref=dst.at[1 - slot],
            send_sem=hs.at[sem, slot],
            recv_sem=hr.at[sem, 1 - slot],
            device_id=(target, dp),
            device_id_type=MESH,
        )

    def send_halos(src, dst, sem):
        @pl.when(me > 0)
        def _():
            halo(src, dst, sem, True).start()

        @pl.when(me < NS - 1)
        def _():
            halo(src, dst, sem, False).start()

    def wait_halos(src, dst, sem):
        @pl.when(me > 0)
        def _():
            halo(src, dst, sem, True).wait_send()
            halo(src, dst, sem, False).wait_recv()

        @pl.when(me < NS - 1)
        def _():
            halo(src, dst, sem, False).wait_send()
            halo(src, dst, sem, True).wait_recv()

    for copy in ld_pm:
        copy.wait()
    for l in range(2):
        raw = pm[l].astype(F32)
        stage[l, pl.ds(8, POS), :] = raw
        zcm[l] = raw - mean(MID + 128 * l, 128)
    for slot, h in ((0, 0), (1, SLAB - 1)):
        for l in range(2):
            zsend[slot, :, l * 128 : l * 128 + 128] = stage[
                l, pl.ds(8 + h, PLANE, stride=SLAB), :
            ].astype(BF16)

    for copy in ld_rm:
        copy.wait()
    for l in range(2):
        rmt[pl.ds(l * 128, 128), :] = rm[l].T

    row = lax.broadcasted_iota(jnp.int32, (PLANE, 128), 0)
    column = lax.rem(row, COLS)
    masks[0] = jnp.where(column == COLS - 1, 0.0, 1.0)
    masks[1] = jnp.where(column == 0, 0.0, 1.0)

    for copy in ld_rf:
        copy.wait()
    for l in range(2):
        stage[l, pl.ds(8, POS), :] = rf[l].astype(F32)
    for h in range(SLAB):
        for l in range(2):
            rfh[pl.ds(h * PLANE, PLANE), l * 128 : l * 128 + 128] = stage[
                l, pl.ds(8 + h, PLANE, stride=SLAB), :
            ].astype(BF16)
    for l in range(2):
        rft[pl.ds(l * 128, 128), :] = rfh[:, l * 128 : l * 128 + 128].T

    for copy in ld_pf:
        copy.wait()
    for l in range(2):
        stage[l, pl.ds(8, POS), :] = pf[l].astype(F32)
    for h in range(SLAB):
        for l in range(2):
            zfh[pl.ds(h * PLANE, PLANE), l * 128 : l * 128 + 128] = stage[
                l, pl.ds(8 + h, PLANE, stride=SLAB), :
            ].astype(BF16)
    for l in range(2):
        stage[l, pl.ds(0, 8), :] = jnp.zeros((8, 128), F32)
        stage[l, pl.ds(8 + POS, 8), :] = jnp.zeros((8, 128), F32)
        for side in range(2):
            hstage[side, l, pl.ds(0, 8), :] = jnp.zeros((8, 128), F32)
            hstage[side, l, pl.ds(8 + PLANE, 8), :] = jnp.zeros((8, 128), F32)

    for copy in ld_wd + ld_bo + ld_pz + ld_wl + ld_wc:
        copy.wait()
    pl.semaphore_wait(near, 2)
    signal(wide, along(2))
    signal(wide, along(6))

    acc[...] = jnp.zeros_like(acc)

    def project(step, carry):
        group = lax.rem(my_group + jnp.where(step == 0, 0, jnp.where(step == 1, 2, jnp.where(step == 2, 3, 1))), 4)
        for q in range(4):
            sender = group * 4 + q

            @pl.when(sender != me)
            def _():
                exchange(sender, sender).wait_recv()

        rows = pl.ds(pl.multiple_of(group * PLANE, PLANE), PLANE)
        for c in range(4):
            up = lax.dot_general(
                recv[rows, :], wd[pl.ds(c * 256, 256), :], NT, preferred_element_type=F32
            )
            for l in range(2):
                j = 2 * c + l
                at = slice(j * 128, j * 128 + 128)
                g = up[:, l * 128 : l * 128 + 128].astype(BF16)
                g = jnp.where(bo[j, rows, :] > 0, g, jnp.zeros_like(g))
                glast[rows, at] = g
                g = g.astype(F32)
                acc[0, :, at] += folded(g)
                acc[1, :, at] += folded(g * pz[j, rows, :].astype(F32))
        return carry

    lax.fori_loop(0, 4, project, 0)

    def share(slots, own, sends, recvs, axis):
        at = me if axis == "space" else dp

        def desc(other, sender):
            return pltpu.make_async_remote_copy(
                src_ref=slots.at[at],
                dst_ref=slots.at[sender],
                send_sem=sends.at[other],
                recv_sem=recvs.at[sender],
                device_id=(other, dp) if axis == "space" else (me, other),
                device_id_type=MESH,
            )

        slots[at] = own

        for k in ORDER:
            desc(lax.rem(at + k, 16), at).start()

        def finish():
            def wait(k, carry):
                other = lax.rem(at + k, 16)
                desc(other, other).wait_recv()
                return carry

            lax.fori_loop(1, 16, wait, 0)
            return jnp.sum(slots[...], axis=0)

        def drain():
            def wait(k, carry):
                desc(lax.rem(at + k, 16), at).wait_send()
                return carry

            lax.fori_loop(1, 16, wait, 0)

        return finish, drain

    def coefficients(sums, lo, n):
        scale = gain(lo, n) * rstd(lo, n)
        crossed = sums[1:2] * rstd(lo, n)
        slope = -scale * rstd(lo, n) * crossed * (1.0 / M)
        shift = -scale * sums[0:1] * (1.0 / M)
        return scale, slope, shift, crossed

    mean1 = mean(2 * MID, CH)

    def local_sums(n, centre):
        total = jnp.sum(acc[0, :, :n], axis=0, keepdims=True)
        product = jnp.sum(acc[1, :, :n], axis=0, keepdims=True)
        return jnp.concatenate([total, product - centre * total], axis=0)

    own = local_sums(CH, mean1)
    finish1, drain1 = share(st1, own, s1s, s1r, "space")
    send_halos(zsend, zhalo, 0)
    pl.semaphore_wait(wide, 2)
    signal(other, across)

    def drain_exchange(k, carry):
        exchange(lax.rem(me + k, NS), me).wait_send()
        return carry

    lax.fori_loop(1, NS, drain_exchange, 0)
    sums1 = finish1()
    scale1, slope1, shift1, crossed1 = coefficients(sums1, 2 * MID, CH)
    shift1 = shift1 - slope1 * mean1

    acc[...] = jnp.zeros_like(acc)

    def middle(step, carry):
        rows = pl.ds(step * PLANE, PLANE)
        for j in range(8):
            at = slice(j * 128, j * 128 + 128)
            z = pz[j, rows, :].astype(F32)
            ldz[rows, at] = (
                glast[rows, at].astype(F32) * scale1[:, at] + z * slope1[:, at] + shift1[:, at]
            ).astype(BF16)
        mi = lax.dot_general(ldz[rows, :], wl[...], NT, preferred_element_type=F32)
        for l in range(2):
            at = slice(l * 128, l * 128 + 128)
            g = jnp.where(rm[l, rows, :].astype(F32) > 0, mi[:, at], 0.0)
            gmid[l, rows, :] = g
            acc[0, :, at] += folded(g)
            acc[1, :, at] += folded(g * zcm[l, rows, :])
        return carry

    for step in range(4):
        middle(step, 0)
    own = local_sums(MID, 0.0)
    finish2, drain2 = share(st2, own, s2s, s2r, "space")
    for slot, h in ((0, 0), (1, SLAB - 1)):
        for l in range(2):
            gsend[slot, :, l * 128 : l * 128 + 128] = gmid[
                l, pl.ds(h, PLANE, stride=SLAB), :
            ].astype(BF16)
    send_halos(gsend, ghalo, 1)
    pl.semaphore_wait(other, 1)
    own = jnp.concatenate([crossed1, sums1[0:1]], axis=0)
    finish_last, drain_last = share(std, own, sds.at[0], sdr.at[0], "dp")
    drain1()

    def last(step, carry):
        cols = pl.ds(step * 256, 256)
        res = jnp.dot(rmt[...], ldz[:, cols], preferred_element_type=F32)
        pflat[0, pl.ds(step, MID, stride=4), :] = res[:, :128]
        pflat[1, pl.ds(step, MID, stride=4), :] = res[:, 128:]
        return carry

    for step in range(4):
        last(step, 0)
    part[pl.ds(9 * MID, CH), :] = lanes(pflat, slice(None)).astype(BF16)

    core = lax.rem(me, 2)
    chip = lax.div(me, 2)
    partner = me + 1 - 2 * core

    def block(q, c):
        return pl.ds(pl.multiple_of((2 * q + c) * SHARE, SHARE), SHARE)

    def pair(q):
        return pltpu.make_async_remote_copy(
            src_ref=part.at[block(q, 1 - core)],
            dst_ref=ra.at[q],
            send_sem=as_.at[q],
            recv_sem=ar_.at[q],
            device_id=(partner, dp),
            device_id_type=MESH,
        )

    def chips(target, sender):
        return pltpu.make_async_remote_copy(
            src_ref=sb.at[target],
            dst_ref=rb.at[sender],
            send_sem=bs_.at[target],
            recv_sem=br_.at[sender],
            device_id=(2 * target + core, dp),
            device_id_type=MESH,
        )

    def start_pairs(lo, hi):
        def go(q, carry):
            pair(q).start()
            return carry

        lax.fori_loop(lo, hi, go, 0)

    def start_chips(lo, hi):
        def go(q, carry):
            pair(q).wait_recv()
            sb[q] = (part[block(q, core), :].astype(F32) + ra[q].astype(F32)).astype(BF16)

            @pl.when(q != chip)
            def _():
                chips(q, chip).start()

            return carry

        lax.fori_loop(lo, hi, go, 0)

    start_pairs(6, 8)

    sums2 = finish2()
    scale2, slope2, shift2, crossed2 = coefficients(sums2, MID, MID)

    for l in range(2):
        at = slice(l * 128, l * 128 + 128)
        stage[l, pl.ds(8, POS), :] = (
            (gmid[l] * scale2[:, at] + zcm[l] * slope2[:, at] + shift2[:, at])
            .astype(BF16)
            .astype(F32)
        )
    for h in range(SLAB):
        for l in range(2):
            for b in (-1, 0, 1):
                x = stage[l, pl.ds(8 + h - SLAB * b, PLANE, stride=SLAB), :]
                if b:
                    x = x * masks[(b + 1) // 2]
                lane = (b + 1) * MID + l * 128
                buf[pl.ds((h + 1) * PLANE, PLANE), lane : lane + 128] = x.astype(BF16)

    wait_halos(zsend, zhalo, 0)
    wait_halos(gsend, ghalo, 1)
    for side in range(2):
        present = me > 0 if side == 0 else me < NS - 1
        for l in range(2):
            at = slice(l * 128, l * 128 + 128)
            z = zhalo[side, :, at].astype(F32) - mean(MID + 128 * l, 128)
            dz = (
                (ghalo[side, :, at].astype(F32) * scale2[:, at] + z * slope2[:, at] + shift2[:, at])
                .astype(BF16)
                .astype(F32)
            )
            hstage[side, l, pl.ds(8, PLANE), :] = jnp.where(present, dz, 0.0)
            for b in (-1, 0, 1):
                x = hstage[side, l, pl.ds(8 - b, PLANE), :]
                if b:
                    x = x * masks[(b + 1) // 2]
                lane = (b + 1) * MID + l * 128
                buf[pl.ds(side * 5 * PLANE, PLANE), lane : lane + 128] = x.astype(BF16)

    drain2()
    start_chips(6, 8)

    def taps(a):
        rows = pl.ds((2 - a) * PLANE, POS)
        for b in range(3):
            part[pl.ds((3 * a + b) * MID, MID), :] = jnp.dot(
                rft[...], buf[rows, b * MID : b * MID + MID], preferred_element_type=F32
            ).astype(BF16)

    taps(0)
    start_pairs(0, 1)
    taps(1)
    start_pairs(1, 3)
    start_chips(0, 1)
    taps(2)
    start_pairs(3, 6)
    start_chips(1, 3)

    acc[...] = jnp.zeros_like(acc)
    mean3 = mean(0, MID)

    def conv(h, carry):
        total = jnp.zeros((PLANE, MID), F32)
        for a in range(3):
            rows = pl.ds((h + 2 - a) * PLANE, PLANE)
            total += lax.dot_general(buf[rows, :], wcat[a], NT, preferred_element_type=F32)
        rows = pl.ds(h * PLANE, PLANE)
        for l in range(2):
            at = slice(l * 128, l * 128 + 128)
            g = jnp.where(rfh[rows, at].astype(F32) > 0, total[:, at], 0.0)
            gfirst[l, pl.ds(h, PLANE, stride=SLAB), :] = g
            z = zfh[rows, at].astype(F32)
            acc[0, :, at] += folded(g)
            acc[1, :, at] += folded(g * z)
        return carry

    for h in range(SLAB):
        conv(h, 0)
        if h == 1:
            start_chips(3, 6)
    own = local_sums(MID, mean3)
    finish3, drain3 = share(st3, own, s3s, s3r, "space")
    ng_ref[:, 2 * MID :] = finish_last() * FACTOR
    drain_last()

    sums3 = finish3()
    scale3, slope3, shift3, crossed3 = coefficients(sums3, 0, MID)
    own = jnp.concatenate(
        [
            jnp.concatenate([crossed3, crossed2], axis=1),
            jnp.concatenate([sums3[0:1], sums2[0:1]], axis=1),
        ],
        axis=0,
    )
    finish4, drain4 = share(st4, own, sds.at[1], sdr.at[1], "dp")
    drain3()

    for l in range(2):
        at = slice(l * 128, l * 128 + 128)
        z = pf[l].astype(F32)
        shift = shift3[:, at] - slope3[:, at] * mean3[:, at]
        ob[l] = (gfirst[l] * scale3[:, at] + z * slope3[:, at] + shift).astype(BF16)
    outs = [
        pltpu.make_async_copy(ob4.at[l], out_hbm.at[:, :, pl.ds(l * 128, 128)], osem.at[l])
        for l in range(2)
    ]
    for copy in outs:
        copy.start()

    tc[pl.ds(0, SHARE), :] = part[block(chip, core), :].astype(F32) + ra[chip].astype(F32)

    def gather(k, carry):
        sender = lax.rem(chip + k, 8)
        chips(sender, sender).wait_recv()
        tc[pl.ds(0, SHARE), :] += rb[sender].astype(F32)
        return carry

    lax.fori_loop(1, 8, gather, 0)
    tc[pl.ds(SHARE, 8), :] = jnp.zeros((8, 256), F32)
    for d in range(ND):
        sc[d] = tc[pl.ds(d * PIECE, 16), :].astype(BF16)
    rc[dp] = sc[dp]

    def shares(target, sender):
        return pltpu.make_async_remote_copy(
            src_ref=sc.at[target],
            dst_ref=rc.at[sender],
            send_sem=cs_.at[target],
            recv_sem=cr_.at[sender],
            device_id=(me, target),
            device_id_type=MESH,
        )

    for k in ORDER:
        shares(lax.rem(dp + k, ND), dp).start()

    def drain_pairs(q, carry):
        pair(q).wait_send()

        @pl.when(q != chip)
        def _():
            chips(q, chip).wait_send()

        return carry

    lax.fori_loop(0, 8, drain_pairs, 0)

    ng_ref[:, : 2 * MID] = finish4() * FACTOR

    def wait(k, carry):
        other = lax.rem(dp + k, ND)
        shares(other, other).wait_recv()
        return carry

    lax.fori_loop(1, ND, wait, 0)
    mine = jnp.sum(rc[...].astype(F32), axis=0) * FACTOR
    for r in range(PIECE):
        wg_ref[2 * r : 2 * r + 1, :] = mine[r : r + 1, :128]
        wg_ref[2 * r + 1 : 2 * r + 2, :] = mine[r : r + 1, 128:]

    drain4()

    def drain_shares(k, carry):
        shares(lax.rem(dp + k, ND), dp).wait_send()
        return carry

    lax.fori_loop(1, ND, drain_shares, 0)
    for copy in outs:
        copy.wait()


def settle(a, b, c, x, y, z, va, vb, vc, sem):
    arrays = ((a, va, x), (b, vb, y), (c, vc, z))
    inward = [pltpu.make_async_copy(src, mid, sem.at[0, i]) for i, (src, mid, _) in enumerate(arrays)]
    outward = [pltpu.make_async_copy(mid, dst, sem.at[1, i]) for i, (_, mid, dst) in enumerate(arrays)]
    for copy in inward:
        copy.start()
    for copy, onward in zip(inward, outward):
        copy.wait()
        onward.start()
    for copy in outward:
        copy.wait()


def shards(
    deep_grad, deep_weight, pre_first, relu_first, pre_middle, relu_middle, pre_last,
    block_output, weight_middle, weight_last, norm_mean, norm_rstd, norm_gain,
):
    def turned(x):
        return jnp.transpose(x, (0, 2, 1, 3)).reshape(PLANE, SLAB, x.shape[-1])

    any_spec = pl.BlockSpec(memory_space=pl.ANY)
    vmem_spec = pl.BlockSpec(memory_space=pltpu.VMEM)
    v = lambda shape, dtype: pltpu.VMEM(shape, dtype)
    dma = lambda *shape: pltpu.SemaphoreType.DMA(shape)
    scratch = [
        v((COLS, ROWS, MID4), BF16),
        v((NS, BLOCK, MID4), BF16),
        v((POS, MID4), BF16),
        v((CH, MID4), BF16),
        v((8, PLANE, SLAB, 128), BF16),
        v((8, PLANE, SLAB, 128), BF16),
        v((2, PLANE, SLAB, 128), BF16),
        v((2, PLANE, SLAB, 128), BF16),
        v((2, PLANE, SLAB, 128), BF16),
        v((2, PLANE, SLAB, 128), BF16),
        v((MID, CH), BF16),
        v((3, MID, 3 * MID), BF16),
        v((POS, CH), BF16),
        v((POS, CH), BF16),
        v((2, POS, 128), F32),
        v((2, POS, 128), F32),
        v((2, POS + 16, 128), F32),
        v((2, 2, PLANE + 16, 128), F32),
        v((6 * PLANE, 3 * MID), BF16),
        v((POS, MID), BF16),
        v((MID, POS), BF16),
        v((MID, POS), BF16),
        v((POS, MID), BF16),
        v((2, POS, 128), F32),
        v((2, PLANE, SLAB, 128), BF16),
        v((2, 8, CH), F32),
        v((NS, 2, CH), F32),
        v((NS, 2, MID), F32),
        v((NS, 2, MID), F32),
        v((ND, 2, 2 * MID), F32),
        v((ND, 2, CH), F32),
        v((2, PLANE, MID), BF16),
        v((2, PLANE, MID), BF16),
        v((2, PLANE, MID), BF16),
        v((2, PLANE, MID), BF16),
        v((2, PLANE, 128), F32),
        v((2, CH, 128), F32),
        v((FLAT, 256), BF16),
        v((8, SHARE, 256), BF16),
        v((8, SHARE, 256), BF16),
        v((8, SHARE, 256), BF16),
        v((SHARE + 8, 256), F32),
        v((ND, 16, 256), BF16),
        v((ND, 16, 256), BF16),
        dma(36), dma(4), dma(2),
        dma(16), dma(16),
        dma(16), dma(16), dma(16), dma(16), dma(16), dma(16), dma(2, 16), dma(2, 16),
        dma(2, 2), dma(2, 2),
        dma(8), dma(8), dma(8), dma(8), dma(16), dma(16),
        pltpu.SemaphoreType.REGULAR, pltpu.SemaphoreType.REGULAR, pltpu.SemaphoreType.REGULAR,
    ]
    first, weights, norms = pl.pallas_call(
        kernel,
        out_shape=(
            jax.ShapeDtypeStruct((PLANE, SLAB, MID), BF16),
            jax.ShapeDtypeStruct((2 * PIECE, 128), F32),
            jax.ShapeDtypeStruct((2, CH + 2 * MID), F32),
        ),
        in_specs=[any_spec] * 10 + [vmem_spec] * 3,
        out_specs=(any_spec, vmem_spec, vmem_spec),
        scratch_shapes=scratch,
        compiler_params=pltpu.CompilerParams(
            collective_id=0, has_side_effects=True, vmem_limit_bytes=60 << 20
        ),
    )(
        jnp.transpose(deep_grad, (0, 2, 1, 3)).reshape(COLS, ROWS, MID4),
        deep_weight,
        turned(pre_first),
        turned(relu_first),
        turned(pre_middle),
        turned(relu_middle),
        turned(pre_last),
        turned(block_output),
        weight_middle,
        weight_last,
        norm_mean,
        norm_rstd,
        norm_gain,
    )
    first, weights, norms = pl.pallas_call(
        settle,
        out_shape=tuple(jax.ShapeDtypeStruct(x.shape, x.dtype) for x in (first, weights, norms)),
        in_specs=[any_spec] * 3,
        out_specs=(any_spec,) * 3,
        scratch_shapes=[v(x.shape, x.dtype) for x in (first, weights, norms)] + [dma(2, 3)],
        compiler_params=pltpu.CompilerParams(vmem_limit_bytes=60 << 20),
    )(first, weights, norms)
    first = jnp.transpose(first.reshape(GROUP, COLS, SLAB, MID), (0, 2, 1, 3))
    return first, weights.reshape(-1), norms


def solution(mesh):
    return jax.shard_map(
        shards,
        mesh=mesh,
        in_specs=(
            P(("dp", "space"), None, None, None),
            P(),
            P("dp", "space", None, None),
            P("dp", "space", None, None),
            P("dp", "space", None, None),
            P("dp", "space", None, None),
            P("dp", "space", None, None),
            P("dp", "space", None, None),
            P(),
            P(),
            P(),
            P(),
            P(),
        ),
        out_specs=(P("dp", "space", None, None), P(("space", "dp")), P()),
        check_vma=False,
    )
```

```python
import functools
import math

import jax
import jax.numpy as jnp
from jax import lax
from jax.experimental import pallas as pl
from jax.experimental.pallas import tpu as pltpu
from jax.sharding import PartitionSpec as P

MESH = pl.DeviceIdType.MESH
F32 = jnp.float32
BF16 = jnp.bfloat16

NS = 16
ND = 16
GROUP = 16
SLAB = 4
COLS = 20
ROWS = 64
CH = 1024
MID = 256
MID4 = 512
POS = GROUP * SLAB * COLS
PLANE = GROUP * COLS
BLOCK = SLAB * COLS
FLAT = 9 * MID + CH
SHARE = FLAT // NS
PIECE = SHARE // ND
M = float(GROUP * ROWS * COLS)
FACTOR = 1.0 / math.sqrt(M * ND)
NT = (((1,), (1,)), ((), ()))
ORDER = (12, 4, 13, 5, 11, 3, 10, 6, 14, 2, 9, 7, 15, 8, 1)


def folded(values):
    return jnp.sum(values.reshape(-1, 8, values.shape[-1]), axis=0)


def lanes(ref, rows):
    return jnp.concatenate([ref[0, rows, :], ref[1, rows, :]], axis=1)


def kernel(
    dg_hbm, wd_hbm, pf_hbm, rf_hbm, pm_hbm, rm_hbm, pz_hbm, bo_hbm, wm_hbm, wl_hbm,
    mean_ref, rstd_ref, gain_ref,
    out_hbm, wg_ref, ng_ref,
    dgv, send, recv, wd, bo4, pz4, pf4, rf4, pm4, rm4, wl, wcat,
    pzd, glast, ldz, zcm, gmid, stage, hstage, buf, rfh, rft, rmt, zfh, gfirst, ob4,
    acc, st1, st2, st3, st4, std,
    zsend, gsend, zhalo, ghalo, masks,
    pflat, part, ra, sb, rb, tc, sc, rc,
    lsem, dsem, osem,
    a2a_s, a2a_r, s1s, s1r, s2s, s2r, s3s, s3r, sds, sdr, hs, hr,
    as_, ar_, bs_, br_, cs_, cr_,
    near, wide, other,
):
    me = lax.axis_index("space")
    dp = lax.axis_index("dp")

    dg_copies = [
        pltpu.make_async_copy(
            dg_hbm.at[:, pl.ds(16 * u, 16), :], dgv.at[:, pl.ds(16 * u, 16), :], dsem.at[u]
        )
        for u in range(4)
    ]
    for copy in dg_copies:
        copy.start()
    loads = []

    def load(src, dst):
        copy = pltpu.make_async_copy(src, dst, lsem.at[len(loads)])
        copy.start()
        loads.append(copy)
        return copy

    def load_tiles(src, dst, count):
        return [load(src.at[:, :, pl.ds(128 * j, 128)], dst.at[j]) for j in range(count)]

    barrier = pltpu.get_barrier_semaphore()

    half, z = lax.div(dp, 8), lax.rem(dp, 8)

    def along(k):
        return (me, half * 8 + lax.rem(z + k, 8))

    across = (me, lax.rem(dp + 8, ND))

    def signal(sem, device):
        pl.semaphore_signal(sem, inc=1, device_id=device, device_id_type=MESH)

    for k in ORDER:
        signal(barrier, (lax.rem(me + k, NS), dp))
    signal(barrier, along(1))
    signal(barrier, along(7))
    signal(barrier, across)

    ld_pm = load_tiles(pm_hbm, pm4, 2)
    ld_rm = load_tiles(rm_hbm, rm4, 2)
    ld_wd = [load(wd_hbm, wd)]
    ld_bo = load_tiles(bo_hbm, bo4, 8)
    ld_pz = load_tiles(pz_hbm, pz4, 8)
    ld_rf = load_tiles(rf_hbm, rf4, 2)
    ld_pf = load_tiles(pf_hbm, pf4, 2)
    ld_wl = [load(wl_hbm, wl)]
    ld_wc = [
        load(wm_hbm.at[pl.ds(t * MID, MID)], wcat.at[t // 3, :, pl.ds((t % 3) * MID, MID)])
        for t in range(9)
    ]

    bo = bo4.reshape(8, POS, 128)
    pz = pz4.reshape(8, POS, 128)
    pf = pf4.reshape(2, POS, 128)
    rf = rf4.reshape(2, POS, 128)
    pm = pm4.reshape(2, POS, 128)
    rm = rm4.reshape(2, POS, 128)
    ob = ob4.reshape(2, POS, 128)

    def exchange(target, sender):
        return pltpu.make_async_remote_copy(
            src_ref=send.at[target],
            dst_ref=recv.at[pl.ds(pl.multiple_of(sender * BLOCK, BLOCK), BLOCK)],
            send_sem=a2a_s.at[target],
            recv_sem=a2a_r.at[sender],
            device_id=(target, dp),
            device_id_type=MESH,
        )

    low = lax.broadcasted_iota(jnp.int32, (10, 8, MID4), 1) < 4
    for u in range(4):
        dg_copies[u].wait()
        x = dgv[:, 16 * u : 16 * u + 16, :].astype(F32)
        for part_ in range(2):
            y = x[:, 8 * part_ : 8 * part_ + 8, :].reshape(10, 2, 8, MID4)
            even, odd = y[:, 0], y[:, 1]
            first = jnp.where(low, even, pltpu.roll(odd, 4, 1))
            second = jnp.where(low, pltpu.roll(even, 4, 1), odd)
            send[u * 4 + 2 * part_] = first.reshape(BLOCK, MID4).astype(BF16)
            send[u * 4 + 2 * part_ + 1] = second.reshape(BLOCK, MID4).astype(BF16)
    pl.semaphore_wait(barrier, NS + 2)
    for k in ORDER:
        exchange(lax.rem(me + k, NS), me).start()
    signal(near, along(1))
    signal(near, along(7))
    recv[pl.ds(pl.multiple_of(me * BLOCK, BLOCK), BLOCK), :] = send[me]

    mean = lambda lo, n: mean_ref[pl.ds(lo, n)].reshape(1, n)
    rstd = lambda lo, n: rstd_ref[pl.ds(lo, n)].reshape(1, n)
    gain = lambda lo, n: gain_ref[pl.ds(lo, n)].reshape(1, n)

    def halo(src, dst, sem, to_up):
        slot = 0 if to_up else 1
        target = lax.rem(me + (NS - 1 if to_up else 1), NS)
        return pltpu.make_async_remote_copy(
            src_ref=src.at[slot],
            dst_ref=dst.at[1 - slot],
            send_sem=hs.at[sem, slot],
            recv_sem=hr.at[sem, 1 - slot],
            device_id=(target, dp),
            device_id_type=MESH,
        )

    def send_halos(src, dst, sem):
        @pl.when(me > 0)
        def _():
            halo(src, dst, sem, True).start()

        @pl.when(me < NS - 1)
        def _():
            halo(src, dst, sem, False).start()

    def wait_halos(src, dst, sem):
        @pl.when(me > 0)
        def _():
            halo(src, dst, sem, True).wait_send()
            halo(src, dst, sem, False).wait_recv()

        @pl.when(me < NS - 1)
        def _():
            halo(src, dst, sem, False).wait_send()
            halo(src, dst, sem, True).wait_recv()

    for copy in ld_pm:
        copy.wait()
    for l in range(2):
        raw = pm[l].astype(F32)
        stage[l, pl.ds(8, POS), :] = raw
        zcm[l] = raw - mean(MID + 128 * l, 128)
    for slot, h in ((0, 0), (1, SLAB - 1)):
        for l in range(2):
            zsend[slot, :, l * 128 : l * 128 + 128] = stage[
                l, pl.ds(8 + h, PLANE, stride=SLAB), :
            ].astype(BF16)

    for copy in ld_rm:
        copy.wait()
    for l in range(2):
        rmt[pl.ds(l * 128, 128), :] = rm[l].T

    row = lax.broadcasted_iota(jnp.int32, (PLANE, 128), 0)
    column = lax.rem(row, COLS)
    masks[0] = jnp.where(column == COLS - 1, 0.0, 1.0)
    masks[1] = jnp.where(column == 0, 0.0, 1.0)

    for copy in ld_rf:
        copy.wait()
    for l in range(2):
        stage[l, pl.ds(8, POS), :] = rf[l].astype(F32)
    for h in range(SLAB):
        for l in range(2):
            rfh[pl.ds(h * PLANE, PLANE), l * 128 : l * 128 + 128] = stage[
                l, pl.ds(8 + h, PLANE, stride=SLAB), :
            ].astype(BF16)
    for l in range(2):
        rft[pl.ds(l * 128, 128), :] = rfh[:, l * 128 : l * 128 + 128].T

    for copy in ld_pf:
        copy.wait()
    for l in range(2):
        stage[l, pl.ds(8, POS), :] = pf[l].astype(F32)
    for h in range(SLAB):
        for l in range(2):
            zfh[pl.ds(h * PLANE, PLANE), l * 128 : l * 128 + 128] = stage[
                l, pl.ds(8 + h, PLANE, stride=SLAB), :
            ].astype(BF16)
    for l in range(2):
        stage[l, pl.ds(0, 8), :] = jnp.zeros((8, 128), F32)
        stage[l, pl.ds(8 + POS, 8), :] = jnp.zeros((8, 128), F32)
        for side in range(2):
            hstage[side, l, pl.ds(0, 8), :] = jnp.zeros((8, 128), F32)
            hstage[side, l, pl.ds(8 + PLANE, 8), :] = jnp.zeros((8, 128), F32)

    for copy in ld_wd + ld_bo + ld_pz + ld_wl + ld_wc:
        copy.wait()
    for j in range(8):
        pzd[:, j * 128 : j * 128 + 128] = pz[j]
    pl.semaphore_wait(near, 2)
    signal(wide, along(2))
    signal(wide, along(6))

    acc[...] = jnp.zeros_like(acc)

    def project(group):
        for q in range(4):
            sender = group * 4 + q

            @pl.when(sender != me)
            def _():
                exchange(sender, sender).wait_recv()

        rows = pl.ds(group * PLANE, PLANE)
        for c in range(4):
            up = lax.dot_general(
                recv[rows, :], wd[pl.ds(c * 256, 256), :], NT, preferred_element_type=F32
            )
            for l in range(2):
                j = 2 * c + l
                at = slice(j * 128, j * 128 + 128)
                g = up[:, l * 128 : l * 128 + 128].astype(BF16)
                g = jnp.where(bo[j, rows, :] > 0, g, jnp.zeros_like(g))
                glast[rows, at] = g
                g = g.astype(F32)
                acc[0, :, at] += folded(g)
                acc[1, :, at] += folded(g * pzd[rows, at].astype(F32))

    for group in range(4):
        project(group)

    def share(slots, own, sends, recvs, axis):
        at = me if axis == "space" else dp

        def desc(other, sender):
            return pltpu.make_async_remote_copy(
                src_ref=slots.at[at],
                dst_ref=slots.at[sender],
                send_sem=sends.at[other],
                recv_sem=recvs.at[sender],
                device_id=(other, dp) if axis == "space" else (me, other),
                device_id_type=MESH,
            )

        slots[at] = own

        for k in ORDER:
            desc(lax.rem(at + k, 16), at).start()

        def finish():
            def wait(k, carry):
                other = lax.rem(at + k, 16)
                desc(other, other).wait_recv()
                return carry

            lax.fori_loop(1, 16, wait, 0)
            return jnp.sum(slots[...], axis=0)

        def drain():
            def wait(k, carry):
                desc(lax.rem(at + k, 16), at).wait_send()
                return carry

            lax.fori_loop(1, 16, wait, 0)

        return finish, drain

    def coefficients(sums, lo, n):
        scale = gain(lo, n) * rstd(lo, n)
        crossed = sums[1:2] * rstd(lo, n)
        slope = -scale * rstd(lo, n) * crossed * (1.0 / M)
        shift = -scale * sums[0:1] * (1.0 / M)
        return scale, slope, shift, crossed

    mean1 = mean(2 * MID, CH)

    def local_sums(n, centre):
        total = jnp.sum(acc[0, :, :n], axis=0, keepdims=True)
        product = jnp.sum(acc[1, :, :n], axis=0, keepdims=True)
        return jnp.concatenate([total, product - centre * total], axis=0)

    own = local_sums(CH, mean1)
    finish1, drain1 = share(st1, own, s1s, s1r, "space")
    send_halos(zsend, zhalo, 0)
    pl.semaphore_wait(wide, 2)
    signal(other, across)

    def drain_exchange(k, carry):
        exchange(lax.rem(me + k, NS), me).wait_send()
        return carry

    lax.fori_loop(1, NS, drain_exchange, 0)
    sums1 = finish1()
    scale1, slope1, shift1, crossed1 = coefficients(sums1, 2 * MID, CH)
    shift1 = shift1 - slope1 * mean1

    acc[...] = jnp.zeros_like(acc)

    def middle(step, carry):
        rows = pl.ds(step * PLANE, PLANE)
        tiles = []
        for j in range(8):
            at = slice(j * 128, j * 128 + 128)
            z = pzd[rows, at].astype(F32)
            dz = glast[rows, at].astype(F32) * scale1[:, at] + z * slope1[:, at] + shift1[:, at]
            tiles.append(dz.astype(BF16))
            ldz[rows, at] = tiles[j]
        mi = lax.dot_general(
            jnp.concatenate(tiles, axis=1), wl[...], NT, preferred_element_type=F32
        )
        for l in range(2):
            at = slice(l * 128, l * 128 + 128)
            g = jnp.where(rm[l, rows, :].astype(F32) > 0, mi[:, at], 0.0)
            gmid[l, rows, :] = g
            acc[0, :, at] += folded(g)
            acc[1, :, at] += folded(g * zcm[l, rows, :])
        return carry

    for step in range(4):
        middle(step, 0)
    own = local_sums(MID, 0.0)
    finish2, drain2 = share(st2, own, s2s, s2r, "space")
    for slot, h in ((0, 0), (1, SLAB - 1)):
        for l in range(2):
            gsend[slot, :, l * 128 : l * 128 + 128] = gmid[
                l, pl.ds(h, PLANE, stride=SLAB), :
            ].astype(BF16)
    send_halos(gsend, ghalo, 1)
    pl.semaphore_wait(other, 1)
    own = jnp.concatenate([crossed1, sums1[0:1]], axis=0)
    finish_last, drain_last = share(std, own, sds.at[0], sdr.at[0], "dp")
    drain1()

    def last(step, carry):
        cols = pl.ds(step * 256, 256)
        res = jnp.dot(rmt[...], ldz[:, cols], preferred_element_type=F32)
        pflat[0, pl.ds(step, MID, stride=4), :] = res[:, :128]
        pflat[1, pl.ds(step, MID, stride=4), :] = res[:, 128:]
        return carry

    for step in range(4):
        last(step, 0)
    part[pl.ds(9 * MID, CH), :] = lanes(pflat, slice(None)).astype(BF16)

    core = lax.rem(me, 2)
    chip = lax.div(me, 2)
    partner = me + 1 - 2 * core

    def block(q, c):
        return pl.ds(pl.multiple_of((2 * q + c) * SHARE, SHARE), SHARE)

    def pair(q):
        return pltpu.make_async_remote_copy(
            src_ref=part.at[block(q, 1 - core)],
            dst_ref=ra.at[q],
            send_sem=as_.at[q],
            recv_sem=ar_.at[q],
            device_id=(partner, dp),
            device_id_type=MESH,
        )

    def chips(target, sender):
        return pltpu.make_async_remote_copy(
            src_ref=sb.at[target],
            dst_ref=rb.at[sender],
            send_sem=bs_.at[target],
            recv_sem=br_.at[sender],
            device_id=(2 * target + core, dp),
            device_id_type=MESH,
        )

    def start_pairs(lo, hi):
        def go(q, carry):
            pair(q).start()
            return carry

        lax.fori_loop(lo, hi, go, 0)

    def start_chips(lo, hi):
        def go(q, carry):
            pair(q).wait_recv()
            sb[q] = (part[block(q, core), :].astype(F32) + ra[q].astype(F32)).astype(BF16)

            @pl.when(q != chip)
            def _():
                chips(q, chip).start()

            return carry

        lax.fori_loop(lo, hi, go, 0)

    start_pairs(6, 8)

    sums2 = finish2()
    scale2, slope2, shift2, crossed2 = coefficients(sums2, MID, MID)

    for l in range(2):
        at = slice(l * 128, l * 128 + 128)
        stage[l, pl.ds(8, POS), :] = (
            (gmid[l] * scale2[:, at] + zcm[l] * slope2[:, at] + shift2[:, at])
            .astype(BF16)
            .astype(F32)
        )
    for h in range(SLAB):
        for l in range(2):
            for b in (-1, 0, 1):
                x = stage[l, pl.ds(8 + h - SLAB * b, PLANE, stride=SLAB), :]
                if b:
                    x = x * masks[(b + 1) // 2]
                lane = (b + 1) * MID + l * 128
                buf[pl.ds((h + 1) * PLANE, PLANE), lane : lane + 128] = x.astype(BF16)

    wait_halos(zsend, zhalo, 0)
    wait_halos(gsend, ghalo, 1)
    for side in range(2):
        present = me > 0 if side == 0 else me < NS - 1
        for l in range(2):
            at = slice(l * 128, l * 128 + 128)
            z = zhalo[side, :, at].astype(F32) - mean(MID + 128 * l, 128)
            dz = (
                (ghalo[side, :, at].astype(F32) * scale2[:, at] + z * slope2[:, at] + shift2[:, at])
                .astype(BF16)
                .astype(F32)
            )
            hstage[side, l, pl.ds(8, PLANE), :] = jnp.where(present, dz, 0.0)
            for b in (-1, 0, 1):
                x = hstage[side, l, pl.ds(8 - b, PLANE), :]
                if b:
                    x = x * masks[(b + 1) // 2]
                lane = (b + 1) * MID + l * 128
                buf[pl.ds(side * 5 * PLANE, PLANE), lane : lane + 128] = x.astype(BF16)

    drain2()
    start_chips(6, 8)

    def taps(a):
        rows = pl.ds((2 - a) * PLANE, POS)
        for b in range(3):
            part[pl.ds((3 * a + b) * MID, MID), :] = jnp.dot(
                rft[...], buf[rows, b * MID : b * MID + MID], preferred_element_type=F32
            ).astype(BF16)

    taps(0)
    start_pairs(0, 1)
    taps(1)
    start_pairs(1, 3)
    start_chips(0, 1)
    taps(2)
    start_pairs(3, 6)
    start_chips(1, 3)

    acc[...] = jnp.zeros_like(acc)
    mean3 = mean(0, MID)

    def conv(h, carry):
        total = jnp.zeros((PLANE, MID), F32)
        for a in range(3):
            rows = pl.ds((h + 2 - a) * PLANE, PLANE)
            total += lax.dot_general(buf[rows, :], wcat[a], NT, preferred_element_type=F32)
        rows = pl.ds(h * PLANE, PLANE)
        for l in range(2):
            at = slice(l * 128, l * 128 + 128)
            g = jnp.where(rfh[rows, at].astype(F32) > 0, total[:, at], 0.0)
            gfirst[l, pl.ds(h, PLANE, stride=SLAB), :] = g
            z = zfh[rows, at].astype(F32)
            acc[0, :, at] += folded(g)
            acc[1, :, at] += folded(g * z)
        return carry

    for h in range(SLAB):
        conv(h, 0)
        if h == 1:
            start_chips(3, 6)
    own = local_sums(MID, mean3)
    finish3, drain3 = share(st3, own, s3s, s3r, "space")
    ng_ref[:, 2 * MID :] = finish_last() * FACTOR
    drain_last()

    sums3 = finish3()
    scale3, slope3, shift3, crossed3 = coefficients(sums3, 0, MID)
    own = jnp.concatenate(
        [
            jnp.concatenate([crossed3, crossed2], axis=1),
            jnp.concatenate([sums3[0:1], sums2[0:1]], axis=1),
        ],
        axis=0,
    )
    finish4, drain4 = share(st4, own, sds.at[1], sdr.at[1], "dp")
    drain3()

    for l in range(2):
        at = slice(l * 128, l * 128 + 128)
        z = pf[l].astype(F32)
        shift = shift3[:, at] - slope3[:, at] * mean3[:, at]
        ob[l] = (gfirst[l] * scale3[:, at] + z * slope3[:, at] + shift).astype(BF16)
    outs = [
        pltpu.make_async_copy(ob4.at[l], out_hbm.at[:, :, pl.ds(l * 128, 128)], osem.at[l])
        for l in range(2)
    ]
    for copy in outs:
        copy.start()

    tc[pl.ds(0, SHARE), :] = part[block(chip, core), :].astype(F32) + ra[chip].astype(F32)

    def gather(k, carry):
        sender = lax.rem(chip + k, 8)
        chips(sender, sender).wait_recv()
        tc[pl.ds(0, SHARE), :] += rb[sender].astype(F32)
        return carry

    lax.fori_loop(1, 8, gather, 0)
    tc[pl.ds(SHARE, 8), :] = jnp.zeros((8, 256), F32)
    for d in range(ND):
        sc[d] = tc[pl.ds(d * PIECE, 16), :].astype(BF16)
    rc[dp] = sc[dp]

    def shares(target, sender):
        return pltpu.make_async_remote_copy(
            src_ref=sc.at[target],
            dst_ref=rc.at[sender],
            send_sem=cs_.at[target],
            recv_sem=cr_.at[sender],
            device_id=(me, target),
            device_id_type=MESH,
        )

    for k in ORDER:
        shares(lax.rem(dp + k, ND), dp).start()

    def drain_pairs(q, carry):
        pair(q).wait_send()

        @pl.when(q != chip)
        def _():
            chips(q, chip).wait_send()

        return carry

    lax.fori_loop(0, 8, drain_pairs, 0)

    ng_ref[:, : 2 * MID] = finish4() * FACTOR

    def wait(k, carry):
        other = lax.rem(dp + k, ND)
        shares(other, other).wait_recv()
        return carry

    lax.fori_loop(1, ND, wait, 0)
    mine = jnp.sum(rc[...].astype(F32), axis=0) * FACTOR
    for r in range(PIECE):
        wg_ref[2 * r : 2 * r + 1, :] = mine[r : r + 1, :128]
        wg_ref[2 * r + 1 : 2 * r + 2, :] = mine[r : r + 1, 128:]

    drain4()

    def drain_shares(k, carry):
        shares(lax.rem(dp + k, ND), dp).wait_send()
        return carry

    lax.fori_loop(1, ND, drain_shares, 0)
    for copy in outs:
        copy.wait()


def settle(a, b, c, x, y, z, va, vb, vc, sem):
    arrays = ((a, va, x), (b, vb, y), (c, vc, z))
    inward = [pltpu.make_async_copy(src, mid, sem.at[0, i]) for i, (src, mid, _) in enumerate(arrays)]
    outward = [pltpu.make_async_copy(mid, dst, sem.at[1, i]) for i, (_, mid, dst) in enumerate(arrays)]
    for copy in inward:
        copy.start()
    for copy, onward in zip(inward, outward):
        copy.wait()
        onward.start()
    for copy in outward:
        copy.wait()


def shards(
    deep_grad, deep_weight, pre_first, relu_first, pre_middle, relu_middle, pre_last,
    block_output, weight_middle, weight_last, norm_mean, norm_rstd, norm_gain,
):
    def turned(x):
        return jnp.transpose(x, (0, 2, 1, 3)).reshape(PLANE, SLAB, x.shape[-1])

    any_spec = pl.BlockSpec(memory_space=pl.ANY)
    vmem_spec = pl.BlockSpec(memory_space=pltpu.VMEM)
    v = lambda shape, dtype: pltpu.VMEM(shape, dtype)
    dma = lambda *shape: pltpu.SemaphoreType.DMA(shape)
    scratch = [
        v((COLS, ROWS, MID4), BF16),
        v((NS, BLOCK, MID4), BF16),
        v((POS, MID4), BF16),
        v((CH, MID4), BF16),
        v((8, PLANE, SLAB, 128), BF16),
        v((8, PLANE, SLAB, 128), BF16),
        v((2, PLANE, SLAB, 128), BF16),
        v((2, PLANE, SLAB, 128), BF16),
        v((2, PLANE, SLAB, 128), BF16),
        v((2, PLANE, SLAB, 128), BF16),
        v((MID, CH), BF16),
        v((3, MID, 3 * MID), BF16),
        v((POS, CH), BF16),
        v((POS, CH), BF16),
        v((POS, CH), BF16),
        v((2, POS, 128), F32),
        v((2, POS, 128), F32),
        v((2, POS + 16, 128), F32),
        v((2, 2, PLANE + 16, 128), F32),
        v((6 * PLANE, 3 * MID), BF16),
        v((POS, MID), BF16),
        v((MID, POS), BF16),
        v((MID, POS), BF16),
        v((POS, MID), BF16),
        v((2, POS, 128), F32),
        v((2, PLANE, SLAB, 128), BF16),
        v((2, 8, CH), F32),
        v((NS, 2, CH), F32),
        v((NS, 2, MID), F32),
        v((NS, 2, MID), F32),
        v((ND, 2, 2 * MID), F32),
        v((ND, 2, CH), F32),
        v((2, PLANE, MID), BF16),
        v((2, PLANE, MID), BF16),
        v((2, PLANE, MID), BF16),
        v((2, PLANE, MID), BF16),
        v((2, PLANE, 128), F32),
        v((2, CH, 128), F32),
        v((FLAT, 256), BF16),
        v((8, SHARE, 256), BF16),
        v((8, SHARE, 256), BF16),
        v((8, SHARE, 256), BF16),
        v((SHARE + 8, 256), F32),
        v((ND, 16, 256), BF16),
        v((ND, 16, 256), BF16),
        dma(36), dma(4), dma(2),
        dma(16), dma(16),
        dma(16), dma(16), dma(16), dma(16), dma(16), dma(16), dma(2, 16), dma(2, 16),
        dma(2, 2), dma(2, 2),
        dma(8), dma(8), dma(8), dma(8), dma(16), dma(16),
        pltpu.SemaphoreType.REGULAR, pltpu.SemaphoreType.REGULAR, pltpu.SemaphoreType.REGULAR,
    ]
    first, weights, norms = pl.pallas_call(
        kernel,
        out_shape=(
            jax.ShapeDtypeStruct((PLANE, SLAB, MID), BF16),
            jax.ShapeDtypeStruct((2 * PIECE, 128), F32),
            jax.ShapeDtypeStruct((2, CH + 2 * MID), F32),
        ),
        in_specs=[any_spec] * 10 + [vmem_spec] * 3,
        out_specs=(any_spec, vmem_spec, vmem_spec),
        scratch_shapes=scratch,
        compiler_params=pltpu.CompilerParams(
            collective_id=0, has_side_effects=True, vmem_limit_bytes=60 << 20
        ),
    )(
        jnp.transpose(deep_grad, (0, 2, 1, 3)).reshape(COLS, ROWS, MID4),
        deep_weight,
        turned(pre_first),
        turned(relu_first),
        turned(pre_middle),
        turned(relu_middle),
        turned(pre_last),
        turned(block_output),
        weight_middle,
        weight_last,
        norm_mean,
        norm_rstd,
        norm_gain,
    )
    first, weights, norms = pl.pallas_call(
        settle,
        out_shape=tuple(jax.ShapeDtypeStruct(x.shape, x.dtype) for x in (first, weights, norms)),
        in_specs=[any_spec] * 3,
        out_specs=(any_spec,) * 3,
        scratch_shapes=[v(x.shape, x.dtype) for x in (first, weights, norms)] + [dma(2, 3)],
        compiler_params=pltpu.CompilerParams(vmem_limit_bytes=60 << 20),
    )(first, weights, norms)
    first = jnp.transpose(first.reshape(GROUP, COLS, SLAB, MID), (0, 2, 1, 3))
    return first, weights.reshape(-1), norms


def solution(mesh):
    return jax.shard_map(
        shards,
        mesh=mesh,
        in_specs=(
            P(("dp", "space"), None, None, None),
            P(),
            P("dp", "space", None, None),
            P("dp", "space", None, None),
            P("dp", "space", None, None),
            P("dp", "space", None, None),
            P("dp", "space", None, None),
            P("dp", "space", None, None),
            P(),
            P(),
            P(),
            P(),
            P(),
        ),
        out_specs=(P("dp", "space", None, None), P(("space", "dp")), P()),
        check_vma=False,
    )
```

```python
import functools
import math

import jax
import jax.numpy as jnp
from jax import lax
from jax.experimental import pallas as pl
from jax.experimental.pallas import tpu as pltpu
from jax.sharding import PartitionSpec as P

MESH = pl.DeviceIdType.MESH
F32 = jnp.float32
BF16 = jnp.bfloat16

NS = 16
ND = 16
GROUP = 16
SLAB = 4
COLS = 20
ROWS = 64
CH = 1024
MID = 256
MID4 = 512
POS = GROUP * SLAB * COLS
PLANE = GROUP * COLS
BLOCK = SLAB * COLS
FLAT = 9 * MID + CH
SHARE = FLAT // NS
PIECE = SHARE // ND
M = float(GROUP * ROWS * COLS)
FACTOR = 1.0 / math.sqrt(M * ND)
NT = (((1,), (1,)), ((), ()))
ORDER = (12, 4, 13, 5, 11, 3, 10, 6, 14, 2, 9, 7, 15, 8, 1)


def folded(values):
    return jnp.sum(values.reshape(-1, 8, values.shape[-1]), axis=0)


def lanes(ref, rows):
    return jnp.concatenate([ref[0, rows, :], ref[1, rows, :]], axis=1)


def kernel(
    dg_hbm, wd_hbm, pf_hbm, rf_hbm, pm_hbm, rm_hbm, pz_hbm, bo_hbm, wm_hbm, wl_hbm,
    mean_ref, rstd_ref, gain_ref,
    out_hbm, wg_ref, ng_ref,
    dgv, send, recv, wd, bo4, pz4, pf4, rf4, pm4, rm4, wl, wcat,
    pzd, glast, ldz, zcm, gmid, stage, hstage, buf, rfh, rft, rmt, zfh, gfirst, ob4,
    acc, st1, st2, st3, st4, std,
    zsend, gsend, zhalo, ghalo, masks,
    pflat, part, ra, sb, rb, tc, sc, rc,
    lsem, dsem, osem,
    a2a_s, a2a_r, s1s, s1r, s2s, s2r, s3s, s3r, sds, sdr, hs, hr,
    as_, ar_, bs_, br_, cs_, cr_,
    near, wide, other,
):
    me = lax.axis_index("space")
    dp = lax.axis_index("dp")

    dg_copies = [
        pltpu.make_async_copy(
            dg_hbm.at[:, pl.ds(16 * u, 16), :], dgv.at[:, pl.ds(16 * u, 16), :], dsem.at[u]
        )
        for u in range(4)
    ]
    for copy in dg_copies:
        copy.start()
    loads = []

    def load(src, dst):
        copy = pltpu.make_async_copy(src, dst, lsem.at[len(loads)])
        copy.start()
        loads.append(copy)
        return copy

    def load_tiles(src, dst, count):
        return [load(src.at[:, :, pl.ds(128 * j, 128)], dst.at[j]) for j in range(count)]

    barrier = pltpu.get_barrier_semaphore()

    half, z = lax.div(dp, 8), lax.rem(dp, 8)

    def along(k):
        return (me, half * 8 + lax.rem(z + k, 8))

    across = (me, lax.rem(dp + 8, ND))

    def signal(sem, device):
        pl.semaphore_signal(sem, inc=1, device_id=device, device_id_type=MESH)

    for k in ORDER:
        signal(barrier, (lax.rem(me + k, NS), dp))
    signal(barrier, along(1))
    signal(barrier, along(7))
    signal(barrier, across)

    ld_pm = load_tiles(pm_hbm, pm4, 2)
    ld_rm = load_tiles(rm_hbm, rm4, 2)
    ld_wd = [load(wd_hbm, wd)]
    ld_bo = load_tiles(bo_hbm, bo4, 8)
    ld_pz = load_tiles(pz_hbm, pz4, 8)
    ld_rf = load_tiles(rf_hbm, rf4, 2)
    ld_pf = load_tiles(pf_hbm, pf4, 2)
    ld_wl = [load(wl_hbm, wl)]
    ld_wc = [
        load(wm_hbm.at[pl.ds(t * MID, MID)], wcat.at[t // 3, :, pl.ds((t % 3) * MID, MID)])
        for t in range(9)
    ]

    bo = bo4.reshape(8, POS, 128)
    pz = pz4.reshape(8, POS, 128)
    pf = pf4.reshape(2, POS, 128)
    rf = rf4.reshape(2, POS, 128)
    pm = pm4.reshape(2, POS, 128)
    rm = rm4.reshape(2, POS, 128)
    ob = ob4.reshape(2, POS, 128)

    def exchange(target, sender):
        return pltpu.make_async_remote_copy(
            src_ref=send.at[target],
            dst_ref=recv.at[pl.ds(pl.multiple_of(sender * BLOCK, BLOCK), BLOCK)],
            send_sem=a2a_s.at[target],
            recv_sem=a2a_r.at[sender],
            device_id=(target, dp),
            device_id_type=MESH,
        )

    low = lax.broadcasted_iota(jnp.int32, (10, 8, MID4), 1) < 4
    for u in range(4):
        dg_copies[u].wait()
        x = dgv[:, 16 * u : 16 * u + 16, :].astype(F32)
        for part_ in range(2):
            y = x[:, 8 * part_ : 8 * part_ + 8, :].reshape(10, 2, 8, MID4)
            even, odd = y[:, 0], y[:, 1]
            first = jnp.where(low, even, pltpu.roll(odd, 4, 1))
            second = jnp.where(low, pltpu.roll(even, 4, 1), odd)
            send[u * 4 + 2 * part_] = first.reshape(BLOCK, MID4).astype(BF16)
            send[u * 4 + 2 * part_ + 1] = second.reshape(BLOCK, MID4).astype(BF16)
    pl.semaphore_wait(barrier, NS + 2)
    for k in ORDER:
        exchange(lax.rem(me + k, NS), me).start()
    signal(near, along(1))
    signal(near, along(7))
    recv[pl.ds(pl.multiple_of(me * BLOCK, BLOCK), BLOCK), :] = send[me]

    mean = lambda lo, n: mean_ref[pl.ds(lo, n)].reshape(1, n)
    rstd = lambda lo, n: rstd_ref[pl.ds(lo, n)].reshape(1, n)
    gain = lambda lo, n: gain_ref[pl.ds(lo, n)].reshape(1, n)

    def halo(src, dst, sem, to_up):
        slot = 0 if to_up else 1
        target = lax.rem(me + (NS - 1 if to_up else 1), NS)
        return pltpu.make_async_remote_copy(
            src_ref=src.at[slot],
            dst_ref=dst.at[1 - slot],
            send_sem=hs.at[sem, slot],
            recv_sem=hr.at[sem, 1 - slot],
            device_id=(target, dp),
            device_id_type=MESH,
        )

    def send_halos(src, dst, sem):
        @pl.when(me > 0)
        def _():
            halo(src, dst, sem, True).start()

        @pl.when(me < NS - 1)
        def _():
            halo(src, dst, sem, False).start()

    def wait_halos(src, dst, sem):
        @pl.when(me > 0)
        def _():
            halo(src, dst, sem, True).wait_send()
            halo(src, dst, sem, False).wait_recv()

        @pl.when(me < NS - 1)
        def _():
            halo(src, dst, sem, False).wait_send()
            halo(src, dst, sem, True).wait_recv()

    for copy in ld_pm:
        copy.wait()
    for l in range(2):
        raw = pm[l].astype(F32)
        stage[l, pl.ds(8, POS), :] = raw
        zcm[l] = raw - mean(MID + 128 * l, 128)
    for slot, h in ((0, 0), (1, SLAB - 1)):
        for l in range(2):
            zsend[slot, :, l * 128 : l * 128 + 128] = stage[
                l, pl.ds(8 + h, PLANE, stride=SLAB), :
            ].astype(BF16)

    for copy in ld_rm:
        copy.wait()
    for l in range(2):
        rmt[pl.ds(l * 128, 128), :] = rm[l].T

    row = lax.broadcasted_iota(jnp.int32, (PLANE, 128), 0)
    column = lax.rem(row, COLS)
    masks[0] = jnp.where(column == COLS - 1, 0.0, 1.0)
    masks[1] = jnp.where(column == 0, 0.0, 1.0)

    for copy in ld_rf:
        copy.wait()
    for l in range(2):
        stage[l, pl.ds(8, POS), :] = rf[l].astype(F32)
    for h in range(SLAB):
        for l in range(2):
            rfh[pl.ds(h * PLANE, PLANE), l * 128 : l * 128 + 128] = stage[
                l, pl.ds(8 + h, PLANE, stride=SLAB), :
            ].astype(BF16)
    for l in range(2):
        rft[pl.ds(l * 128, 128), :] = rfh[:, l * 128 : l * 128 + 128].T

    for copy in ld_pf:
        copy.wait()
    for l in range(2):
        stage[l, pl.ds(8, POS), :] = pf[l].astype(F32)
    for h in range(SLAB):
        for l in range(2):
            zfh[pl.ds(h * PLANE, PLANE), l * 128 : l * 128 + 128] = stage[
                l, pl.ds(8 + h, PLANE, stride=SLAB), :
            ].astype(BF16)
    for l in range(2):
        stage[l, pl.ds(0, 8), :] = jnp.zeros((8, 128), F32)
        stage[l, pl.ds(8 + POS, 8), :] = jnp.zeros((8, 128), F32)
        for side in range(2):
            hstage[side, l, pl.ds(0, 8), :] = jnp.zeros((8, 128), F32)
            hstage[side, l, pl.ds(8 + PLANE, 8), :] = jnp.zeros((8, 128), F32)

    for copy in ld_wd + ld_bo + ld_pz + ld_wl + ld_wc:
        copy.wait()
    for j in range(8):
        pzd[:, j * 128 : j * 128 + 128] = pz[j]
    pl.semaphore_wait(near, 2)
    signal(wide, along(2))
    signal(wide, along(6))

    acc[...] = jnp.zeros_like(acc)

    def project(group):
        for q in range(4):
            sender = group * 4 + q

            @pl.when(sender != me)
            def _():
                exchange(sender, sender).wait_recv()

        rows = pl.ds(group * PLANE, PLANE)
        for c in range(4):
            up = lax.dot_general(
                recv[rows, :], wd[pl.ds(c * 256, 256), :], NT, preferred_element_type=F32
            )
            for l in range(2):
                j = 2 * c + l
                at = slice(j * 128, j * 128 + 128)
                g = up[:, l * 128 : l * 128 + 128].astype(BF16)
                g = jnp.where(bo[j, rows, :] > 0, g, jnp.zeros_like(g))
                glast[rows, at] = g
                g = g.astype(F32)
                acc[0, :, at] += folded(g)
                acc[1, :, at] += folded(g * pzd[rows, at].astype(F32))

    for group in range(4):
        project(group)

    def share(slots, own, sends, recvs, axis):
        at = me if axis == "space" else dp

        def desc(other, sender):
            return pltpu.make_async_remote_copy(
                src_ref=slots.at[at],
                dst_ref=slots.at[sender],
                send_sem=sends.at[other],
                recv_sem=recvs.at[sender],
                device_id=(other, dp) if axis == "space" else (me, other),
                device_id_type=MESH,
            )

        slots[at] = own

        for k in ORDER:
            desc(lax.rem(at + k, 16), at).start()

        def finish():
            def wait(k, carry):
                other = lax.rem(at + k, 16)
                desc(other, other).wait_recv()
                return carry

            lax.fori_loop(1, 16, wait, 0)
            return jnp.sum(slots[...], axis=0)

        def drain():
            def wait(k, carry):
                desc(lax.rem(at + k, 16), at).wait_send()
                return carry

            lax.fori_loop(1, 16, wait, 0)

        return finish, drain

    def coefficients(sums, lo, n):
        scale = gain(lo, n) * rstd(lo, n)
        crossed = sums[1:2] * rstd(lo, n)
        slope = -scale * rstd(lo, n) * crossed * (1.0 / M)
        shift = -scale * sums[0:1] * (1.0 / M)
        return scale, slope, shift, crossed

    mean1 = mean(2 * MID, CH)

    def local_sums(n, centre):
        total = jnp.sum(acc[0, :, :n], axis=0, keepdims=True)
        product = jnp.sum(acc[1, :, :n], axis=0, keepdims=True)
        return jnp.concatenate([total, product - centre * total], axis=0)

    own = local_sums(CH, mean1)
    finish1, drain1 = share(st1, own, s1s, s1r, "space")
    send_halos(zsend, zhalo, 0)
    pl.semaphore_wait(wide, 2)
    signal(other, across)

    def drain_exchange(k, carry):
        exchange(lax.rem(me + k, NS), me).wait_send()
        return carry

    lax.fori_loop(1, NS, drain_exchange, 0)
    sums1 = finish1()
    scale1, slope1, shift1, crossed1 = coefficients(sums1, 2 * MID, CH)
    shift1 = shift1 - slope1 * mean1

    acc[...] = jnp.zeros_like(acc)

    def middle(step, carry):
        rows = pl.ds(step * PLANE, PLANE)
        tiles = []
        for j in range(8):
            at = slice(j * 128, j * 128 + 128)
            z = pzd[rows, at].astype(F32)
            dz = glast[rows, at].astype(F32) * scale1[:, at] + z * slope1[:, at] + shift1[:, at]
            tiles.append(dz.astype(BF16))
            ldz[rows, at] = tiles[j]
        mi = lax.dot_general(
            jnp.concatenate(tiles, axis=1), wl[...], NT, preferred_element_type=F32
        )
        for l in range(2):
            at = slice(l * 128, l * 128 + 128)
            g = jnp.where(rm[l, rows, :].astype(F32) > 0, mi[:, at], 0.0)
            gmid[l, rows, :] = g
            acc[0, :, at] += folded(g)
            acc[1, :, at] += folded(g * zcm[l, rows, :])
        return carry

    for step in range(4):
        middle(step, 0)
    own = local_sums(MID, 0.0)
    finish2, drain2 = share(st2, own, s2s, s2r, "space")
    for slot, h in ((0, 0), (1, SLAB - 1)):
        for l in range(2):
            gsend[slot, :, l * 128 : l * 128 + 128] = gmid[
                l, pl.ds(h, PLANE, stride=SLAB), :
            ].astype(BF16)
    send_halos(gsend, ghalo, 1)
    norm_last = jnp.concatenate([crossed1, sums1[0:1]], axis=0)

    def last(step, carry):
        cols = pl.ds(step * 256, 256)
        res = jnp.dot(rmt[...], ldz[:, cols], preferred_element_type=F32)
        pflat[0, pl.ds(step, MID, stride=4), :] = res[:, :128]
        pflat[1, pl.ds(step, MID, stride=4), :] = res[:, 128:]
        return carry

    for step in range(4):
        last(step, 0)
    part[pl.ds(9 * MID, CH), :] = lanes(pflat, slice(None)).astype(BF16)

    core = lax.rem(me, 2)
    chip = lax.div(me, 2)
    partner = me + 1 - 2 * core

    def block(q, c):
        return pl.ds(pl.multiple_of((2 * q + c) * SHARE, SHARE), SHARE)

    def pair(q):
        return pltpu.make_async_remote_copy(
            src_ref=part.at[block(q, 1 - core)],
            dst_ref=ra.at[q],
            send_sem=as_.at[q],
            recv_sem=ar_.at[q],
            device_id=(partner, dp),
            device_id_type=MESH,
        )

    def chips(target, sender):
        return pltpu.make_async_remote_copy(
            src_ref=sb.at[target],
            dst_ref=rb.at[sender],
            send_sem=bs_.at[target],
            recv_sem=br_.at[sender],
            device_id=(2 * target + core, dp),
            device_id_type=MESH,
        )

    def start_pairs(lo, hi):
        def go(q, carry):
            pair(q).start()
            return carry

        lax.fori_loop(lo, hi, go, 0)

    def start_chips(lo, hi):
        def go(q, carry):
            pair(q).wait_recv()
            sb[q] = (part[block(q, core), :].astype(F32) + ra[q].astype(F32)).astype(BF16)

            @pl.when(q != chip)
            def _():
                chips(q, chip).start()

            return carry

        lax.fori_loop(lo, hi, go, 0)

    start_pairs(6, 8)
    start_chips(6, 8)
    sums2 = finish2()
    scale2, slope2, shift2, crossed2 = coefficients(sums2, MID, MID)

    for l in range(2):
        at = slice(l * 128, l * 128 + 128)
        stage[l, pl.ds(8, POS), :] = (
            (gmid[l] * scale2[:, at] + zcm[l] * slope2[:, at] + shift2[:, at])
            .astype(BF16)
            .astype(F32)
        )
    for h in range(SLAB):
        for l in range(2):
            for b in (-1, 0, 1):
                x = stage[l, pl.ds(8 + h - SLAB * b, PLANE, stride=SLAB), :]
                if b:
                    x = x * masks[(b + 1) // 2]
                lane = (b + 1) * MID + l * 128
                buf[pl.ds((h + 1) * PLANE, PLANE), lane : lane + 128] = x.astype(BF16)

    wait_halos(zsend, zhalo, 0)
    wait_halos(gsend, ghalo, 1)
    for side in range(2):
        present = me > 0 if side == 0 else me < NS - 1
        for l in range(2):
            at = slice(l * 128, l * 128 + 128)
            z = zhalo[side, :, at].astype(F32) - mean(MID + 128 * l, 128)
            dz = (
                (ghalo[side, :, at].astype(F32) * scale2[:, at] + z * slope2[:, at] + shift2[:, at])
                .astype(BF16)
                .astype(F32)
            )
            hstage[side, l, pl.ds(8, PLANE), :] = jnp.where(present, dz, 0.0)
            for b in (-1, 0, 1):
                x = hstage[side, l, pl.ds(8 - b, PLANE), :]
                if b:
                    x = x * masks[(b + 1) // 2]
                lane = (b + 1) * MID + l * 128
                buf[pl.ds(side * 5 * PLANE, PLANE), lane : lane + 128] = x.astype(BF16)


    def taps(a):
        rows = pl.ds((2 - a) * PLANE, POS)
        for b in range(3):
            part[pl.ds((3 * a + b) * MID, MID), :] = jnp.dot(
                rft[...], buf[rows, b * MID : b * MID + MID], preferred_element_type=F32
            ).astype(BF16)

    taps(0)
    start_pairs(0, 1)
    taps(1)
    start_pairs(1, 3)
    start_chips(0, 1)
    taps(2)
    start_pairs(3, 6)
    start_chips(1, 3)

    acc[...] = jnp.zeros_like(acc)
    mean3 = mean(0, MID)

    def conv(h, carry):
        total = jnp.zeros((PLANE, MID), F32)
        for a in range(3):
            rows = pl.ds((h + 2 - a) * PLANE, PLANE)
            total += lax.dot_general(buf[rows, :], wcat[a], NT, preferred_element_type=F32)
        rows = pl.ds(h * PLANE, PLANE)
        for l in range(2):
            at = slice(l * 128, l * 128 + 128)
            g = jnp.where(rfh[rows, at].astype(F32) > 0, total[:, at], 0.0)
            gfirst[l, pl.ds(h, PLANE, stride=SLAB), :] = g
            z = zfh[rows, at].astype(F32)
            acc[0, :, at] += folded(g)
            acc[1, :, at] += folded(g * z)
        return carry

    for h in range(SLAB):
        conv(h, 0)
        if h == 0:
            start_chips(3, 6)
    own = local_sums(MID, mean3)
    finish3, drain3 = share(st3, own, s3s, s3r, "space")
    pl.semaphore_wait(other, 1)
    finish_last, drain_last = share(std, norm_last, sds.at[0], sdr.at[0], "dp")
    drain1()
    drain2()

    sums3 = finish3()
    scale3, slope3, shift3, crossed3 = coefficients(sums3, 0, MID)
    own = jnp.concatenate(
        [
            jnp.concatenate([crossed3, crossed2], axis=1),
            jnp.concatenate([sums3[0:1], sums2[0:1]], axis=1),
        ],
        axis=0,
    )
    finish4, drain4 = share(st4, own, sds.at[1], sdr.at[1], "dp")
    drain3()

    for l in range(2):
        at = slice(l * 128, l * 128 + 128)
        z = pf[l].astype(F32)
        shift = shift3[:, at] - slope3[:, at] * mean3[:, at]
        ob[l] = (gfirst[l] * scale3[:, at] + z * slope3[:, at] + shift).astype(BF16)
    outs = [
        pltpu.make_async_copy(ob4.at[l], out_hbm.at[:, :, pl.ds(l * 128, 128)], osem.at[l])
        for l in range(2)
    ]
    for copy in outs:
        copy.start()

    tc[pl.ds(0, SHARE), :] = part[block(chip, core), :].astype(F32) + ra[chip].astype(F32)

    def gather(k, carry):
        sender = lax.rem(chip + k, 8)
        chips(sender, sender).wait_recv()
        tc[pl.ds(0, SHARE), :] += rb[sender].astype(F32)
        return carry

    lax.fori_loop(1, 8, gather, 0)
    tc[pl.ds(SHARE, 8), :] = jnp.zeros((8, 256), F32)
    for d in range(ND):
        sc[d] = tc[pl.ds(d * PIECE, 16), :].astype(BF16)
    rc[dp] = sc[dp]

    def shares(target, sender):
        return pltpu.make_async_remote_copy(
            src_ref=sc.at[target],
            dst_ref=rc.at[sender],
            send_sem=cs_.at[target],
            recv_sem=cr_.at[sender],
            device_id=(me, target),
            device_id_type=MESH,
        )

    for k in ORDER:
        shares(lax.rem(dp + k, ND), dp).start()

    def drain_pairs(q, carry):
        pair(q).wait_send()

        @pl.when(q != chip)
        def _():
            chips(q, chip).wait_send()

        return carry

    lax.fori_loop(0, 8, drain_pairs, 0)

    ng_ref[:, 2 * MID :] = finish_last() * FACTOR
    drain_last()
    ng_ref[:, : 2 * MID] = finish4() * FACTOR
    drain4()

    def drain_shares(k, carry):
        shares(lax.rem(dp + k, ND), dp).wait_send()
        return carry

    lax.fori_loop(1, ND, drain_shares, 0)
    for copy in outs:
        copy.wait()

    def wait(k, carry):
        sender = lax.rem(dp + k, ND)
        shares(sender, sender).wait_recv()
        return carry

    lax.fori_loop(1, ND, wait, 0)
    mine = jnp.sum(rc[...].astype(F32), axis=0) * FACTOR
    for r in range(PIECE):
        wg_ref[2 * r : 2 * r + 1, :] = mine[r : r + 1, :128]
        wg_ref[2 * r + 1 : 2 * r + 2, :] = mine[r : r + 1, 128:]


def settle(a, b, c, x, y, z, va, vb, vc, sem):
    arrays = ((a, va, x), (b, vb, y), (c, vc, z))
    inward = [pltpu.make_async_copy(src, mid, sem.at[0, i]) for i, (src, mid, _) in enumerate(arrays)]
    outward = [pltpu.make_async_copy(mid, dst, sem.at[1, i]) for i, (_, mid, dst) in enumerate(arrays)]
    for copy in inward:
        copy.start()
    for copy, onward in zip(inward, outward):
        copy.wait()
        onward.start()
    for copy in outward:
        copy.wait()


def shards(
    deep_grad, deep_weight, pre_first, relu_first, pre_middle, relu_middle, pre_last,
    block_output, weight_middle, weight_last, norm_mean, norm_rstd, norm_gain,
):
    def turned(x):
        return jnp.transpose(x, (0, 2, 1, 3)).reshape(PLANE, SLAB, x.shape[-1])

    any_spec = pl.BlockSpec(memory_space=pl.ANY)
    vmem_spec = pl.BlockSpec(memory_space=pltpu.VMEM)
    v = lambda shape, dtype: pltpu.VMEM(shape, dtype)
    dma = lambda *shape: pltpu.SemaphoreType.DMA(shape)
    scratch = [
        v((COLS, ROWS, MID4), BF16),
        v((NS, BLOCK, MID4), BF16),
        v((POS, MID4), BF16),
        v((CH, MID4), BF16),
        v((8, PLANE, SLAB, 128), BF16),
        v((8, PLANE, SLAB, 128), BF16),
        v((2, PLANE, SLAB, 128), BF16),
        v((2, PLANE, SLAB, 128), BF16),
        v((2, PLANE, SLAB, 128), BF16),
        v((2, PLANE, SLAB, 128), BF16),
        v((MID, CH), BF16),
        v((3, MID, 3 * MID), BF16),
        v((POS, CH), BF16),
        v((POS, CH), BF16),
        v((POS, CH), BF16),
        v((2, POS, 128), F32),
        v((2, POS, 128), F32),
        v((2, POS + 16, 128), F32),
        v((2, 2, PLANE + 16, 128), F32),
        v((6 * PLANE, 3 * MID), BF16),
        v((POS, MID), BF16),
        v((MID, POS), BF16),
        v((MID, POS), BF16),
        v((POS, MID), BF16),
        v((2, POS, 128), F32),
        v((2, PLANE, SLAB, 128), BF16),
        v((2, 8, CH), F32),
        v((NS, 2, CH), F32),
        v((NS, 2, MID), F32),
        v((NS, 2, MID), F32),
        v((ND, 2, 2 * MID), F32),
        v((ND, 2, CH), F32),
        v((2, PLANE, MID), BF16),
        v((2, PLANE, MID), BF16),
        v((2, PLANE, MID), BF16),
        v((2, PLANE, MID), BF16),
        v((2, PLANE, 128), F32),
        v((2, CH, 128), F32),
        v((FLAT, 256), BF16),
        v((8, SHARE, 256), BF16),
        v((8, SHARE, 256), BF16),
        v((8, SHARE, 256), BF16),
        v((SHARE + 8, 256), F32),
        v((ND, 16, 256), BF16),
        v((ND, 16, 256), BF16),
        dma(36), dma(4), dma(2),
        dma(16), dma(16),
        dma(16), dma(16), dma(16), dma(16), dma(16), dma(16), dma(2, 16), dma(2, 16),
        dma(2, 2), dma(2, 2),
        dma(8), dma(8), dma(8), dma(8), dma(16), dma(16),
        pltpu.SemaphoreType.REGULAR, pltpu.SemaphoreType.REGULAR, pltpu.SemaphoreType.REGULAR,
    ]
    first, weights, norms = pl.pallas_call(
        kernel,
        out_shape=(
            jax.ShapeDtypeStruct((PLANE, SLAB, MID), BF16),
            jax.ShapeDtypeStruct((2 * PIECE, 128), F32),
            jax.ShapeDtypeStruct((2, CH + 2 * MID), F32),
        ),
        in_specs=[any_spec] * 10 + [vmem_spec] * 3,
        out_specs=(any_spec, vmem_spec, vmem_spec),
        scratch_shapes=scratch,
        compiler_params=pltpu.CompilerParams(
            collective_id=0, has_side_effects=True, vmem_limit_bytes=60 << 20
        ),
    )(
        jnp.transpose(deep_grad, (0, 2, 1, 3)).reshape(COLS, ROWS, MID4),
        deep_weight,
        turned(pre_first),
        turned(relu_first),
        turned(pre_middle),
        turned(relu_middle),
        turned(pre_last),
        turned(block_output),
        weight_middle,
        weight_last,
        norm_mean,
        norm_rstd,
        norm_gain,
    )
    first, weights, norms = pl.pallas_call(
        settle,
        out_shape=tuple(jax.ShapeDtypeStruct(x.shape, x.dtype) for x in (first, weights, norms)),
        in_specs=[any_spec] * 3,
        out_specs=(any_spec,) * 3,
        scratch_shapes=[v(x.shape, x.dtype) for x in (first, weights, norms)] + [dma(2, 3)],
        compiler_params=pltpu.CompilerParams(vmem_limit_bytes=60 << 20),
    )(first, weights, norms)
    first = jnp.transpose(first.reshape(GROUP, COLS, SLAB, MID), (0, 2, 1, 3))
    return first, weights.reshape(-1), norms


def solution(mesh):
    return jax.shard_map(
        shards,
        mesh=mesh,
        in_specs=(
            P(("dp", "space"), None, None, None),
            P(),
            P("dp", "space", None, None),
            P("dp", "space", None, None),
            P("dp", "space", None, None),
            P("dp", "space", None, None),
            P("dp", "space", None, None),
            P("dp", "space", None, None),
            P(),
            P(),
            P(),
            P(),
            P(),
        ),
        out_specs=(P("dp", "space", None, None), P(("space", "dp")), P()),
        check_vma=False,
    )
```

```python
import functools
import math

import jax
import jax.numpy as jnp
from jax import lax
from jax.experimental import pallas as pl
from jax.experimental.pallas import tpu as pltpu
from jax.sharding import PartitionSpec as P

MESH = pl.DeviceIdType.MESH
F32 = jnp.float32
BF16 = jnp.bfloat16

NS = 16
ND = 16
GROUP = 16
SLAB = 4
COLS = 20
ROWS = 64
CH = 1024
MID = 256
MID4 = 512
POS = GROUP * SLAB * COLS
PLANE = GROUP * COLS
BLOCK = SLAB * COLS
FLAT = 9 * MID + CH
SHARE = FLAT // NS
PIECE = SHARE // ND
M = float(GROUP * ROWS * COLS)
FACTOR = 1.0 / math.sqrt(M * ND)
NT = (((1,), (1,)), ((), ()))
ORDER = (12, 4, 13, 5, 11, 3, 10, 6, 14, 2, 9, 7, 15, 8, 1)


def folded(values):
    return jnp.sum(values.reshape(-1, 8, values.shape[-1]), axis=0)


def lanes(ref, rows):
    return jnp.concatenate([ref[0, rows, :], ref[1, rows, :]], axis=1)


def kernel(
    dg_hbm, wd_hbm, pf_hbm, rf_hbm, pm_hbm, rm_hbm, pz_hbm, bo_hbm, wm_hbm, wl_hbm,
    mean_ref, rstd_ref, gain_ref,
    out_hbm, wg_ref, ng_ref,
    dgv, send, recv, wd, bo4, pz4, pf4, rf4, pm4, rm4, wl, wcat,
    pzd, glast, ldz, zcm, gmid, stage, hstage, buf, rfh, rft, rmt, zfh, gfirst, ob4,
    acc, st1, st2, st3, st4, std,
    zsend, gsend, zhalo, ghalo, masks,
    pflat, part, ra, sb, rb, tc, sc, rc,
    lsem, dsem, osem,
    a2a_s, a2a_r, s1s, s1r, s2s, s2r, s3s, s3r, sds, sdr, hs, hr,
    as_, ar_, bs_, br_, cs_, cr_,
    near, wide, other,
):
    me = lax.axis_index("space")
    dp = lax.axis_index("dp")

    dg_copies = [
        pltpu.make_async_copy(
            dg_hbm.at[:, pl.ds(16 * u, 16), :], dgv.at[:, pl.ds(16 * u, 16), :], dsem.at[u]
        )
        for u in range(4)
    ]
    for copy in dg_copies:
        copy.start()
    loads = []

    def load(src, dst):
        copy = pltpu.make_async_copy(src, dst, lsem.at[len(loads)])
        copy.start()
        loads.append(copy)
        return copy

    def load_tiles(src, dst, count):
        return [load(src.at[:, :, pl.ds(128 * j, 128)], dst.at[j]) for j in range(count)]

    barrier = pltpu.get_barrier_semaphore()

    half, z = lax.div(dp, 8), lax.rem(dp, 8)

    def along(k):
        return (me, half * 8 + lax.rem(z + k, 8))

    across = (me, lax.rem(dp + 8, ND))

    def signal(sem, device):
        pl.semaphore_signal(sem, inc=1, device_id=device, device_id_type=MESH)

    for k in ORDER:
        signal(barrier, (lax.rem(me + k, NS), dp))
    signal(barrier, along(1))
    signal(barrier, along(7))
    signal(barrier, across)

    ld_pm = load_tiles(pm_hbm, pm4, 2)
    ld_rm = load_tiles(rm_hbm, rm4, 2)
    ld_wd = [load(wd_hbm, wd)]
    ld_bo = load_tiles(bo_hbm, bo4, 8)
    ld_pz = load_tiles(pz_hbm, pz4, 8)
    ld_rf = load_tiles(rf_hbm, rf4, 2)
    ld_pf = load_tiles(pf_hbm, pf4, 2)
    ld_wl = [load(wl_hbm, wl)]
    ld_wc = [
        load(wm_hbm.at[pl.ds(t * MID, MID)], wcat.at[t // 3, :, pl.ds((t % 3) * MID, MID)])
        for t in range(9)
    ]

    bo = bo4.reshape(8, POS, 128)
    pz = pz4.reshape(8, POS, 128)
    pf = pf4.reshape(2, POS, 128)
    rf = rf4.reshape(2, POS, 128)
    pm = pm4.reshape(2, POS, 128)
    rm = rm4.reshape(2, POS, 128)
    ob = ob4.reshape(2, POS, 128)

    def exchange(target, sender):
        return pltpu.make_async_remote_copy(
            src_ref=send.at[target],
            dst_ref=recv.at[pl.ds(pl.multiple_of(sender * BLOCK, BLOCK), BLOCK)],
            send_sem=a2a_s.at[target],
            recv_sem=a2a_r.at[sender],
            device_id=(target, dp),
            device_id_type=MESH,
        )

    low = lax.broadcasted_iota(jnp.int32, (10, 8, MID4), 1) < 4
    for u in range(4):
        dg_copies[u].wait()
        x = dgv[:, 16 * u : 16 * u + 16, :].astype(F32)
        for part_ in range(2):
            y = x[:, 8 * part_ : 8 * part_ + 8, :].reshape(10, 2, 8, MID4)
            even, odd = y[:, 0], y[:, 1]
            first = jnp.where(low, even, pltpu.roll(odd, 4, 1))
            second = jnp.where(low, pltpu.roll(even, 4, 1), odd)
            send[u * 4 + 2 * part_] = first.reshape(BLOCK, MID4).astype(BF16)
            send[u * 4 + 2 * part_ + 1] = second.reshape(BLOCK, MID4).astype(BF16)
    pl.semaphore_wait(barrier, NS + 2)
    for k in ORDER:
        exchange(lax.rem(me + k, NS), me).start()
    signal(near, along(1))
    signal(near, along(7))
    recv[pl.ds(pl.multiple_of(me * BLOCK, BLOCK), BLOCK), :] = send[me]

    mean = lambda lo, n: mean_ref[pl.ds(lo, n)].reshape(1, n)
    rstd = lambda lo, n: rstd_ref[pl.ds(lo, n)].reshape(1, n)
    gain = lambda lo, n: gain_ref[pl.ds(lo, n)].reshape(1, n)

    def halo(src, dst, sem, to_up):
        slot = 0 if to_up else 1
        target = lax.rem(me + (NS - 1 if to_up else 1), NS)
        return pltpu.make_async_remote_copy(
            src_ref=src.at[slot],
            dst_ref=dst.at[1 - slot],
            send_sem=hs.at[sem, slot],
            recv_sem=hr.at[sem, 1 - slot],
            device_id=(target, dp),
            device_id_type=MESH,
        )

    def send_halos(src, dst, sem):
        @pl.when(me > 0)
        def _():
            halo(src, dst, sem, True).start()

        @pl.when(me < NS - 1)
        def _():
            halo(src, dst, sem, False).start()

    def wait_halos(src, dst, sem):
        @pl.when(me > 0)
        def _():
            halo(src, dst, sem, True).wait_send()
            halo(src, dst, sem, False).wait_recv()

        @pl.when(me < NS - 1)
        def _():
            halo(src, dst, sem, False).wait_send()
            halo(src, dst, sem, True).wait_recv()

    for copy in ld_pm:
        copy.wait()
    for l in range(2):
        raw = pm[l].astype(F32)
        stage[l, pl.ds(8, POS), :] = raw
        zcm[l] = raw - mean(MID + 128 * l, 128)
    for slot, h in ((0, 0), (1, SLAB - 1)):
        for l in range(2):
            zsend[slot, :, l * 128 : l * 128 + 128] = stage[
                l, pl.ds(8 + h, PLANE, stride=SLAB), :
            ].astype(BF16)

    for copy in ld_rm:
        copy.wait()
    for l in range(2):
        rmt[pl.ds(l * 128, 128), :] = rm[l].T

    row = lax.broadcasted_iota(jnp.int32, (PLANE, 128), 0)
    column = lax.rem(row, COLS)
    masks[0] = jnp.where(column == COLS - 1, 0.0, 1.0)
    masks[1] = jnp.where(column == 0, 0.0, 1.0)

    for copy in ld_rf:
        copy.wait()
    for l in range(2):
        stage[l, pl.ds(8, POS), :] = rf[l].astype(F32)
    for h in range(SLAB):
        for l in range(2):
            rfh[pl.ds(h * PLANE, PLANE), l * 128 : l * 128 + 128] = stage[
                l, pl.ds(8 + h, PLANE, stride=SLAB), :
            ].astype(BF16)
    for l in range(2):
        rft[pl.ds(l * 128, 128), :] = rfh[:, l * 128 : l * 128 + 128].T

    for copy in ld_pf:
        copy.wait()
    for l in range(2):
        stage[l, pl.ds(8, POS), :] = pf[l].astype(F32)
    for h in range(SLAB):
        for l in range(2):
            zfh[pl.ds(h * PLANE, PLANE), l * 128 : l * 128 + 128] = stage[
                l, pl.ds(8 + h, PLANE, stride=SLAB), :
            ].astype(BF16)
    for l in range(2):
        stage[l, pl.ds(0, 8), :] = jnp.zeros((8, 128), F32)
        stage[l, pl.ds(8 + POS, 8), :] = jnp.zeros((8, 128), F32)
        for side in range(2):
            hstage[side, l, pl.ds(0, 8), :] = jnp.zeros((8, 128), F32)
            hstage[side, l, pl.ds(8 + PLANE, 8), :] = jnp.zeros((8, 128), F32)

    for copy in ld_wd + ld_bo + ld_pz + ld_wl + ld_wc:
        copy.wait()
    for j in range(8):
        pzd[:, j * 128 : j * 128 + 128] = pz[j]
    pl.semaphore_wait(near, 2)
    signal(wide, along(2))
    signal(wide, along(6))

    acc[...] = jnp.zeros_like(acc)

    def project(group):
        for q in range(4):
            sender = group * 4 + q

            @pl.when(sender != me)
            def _():
                exchange(sender, sender).wait_recv()

        rows = pl.ds(group * PLANE, PLANE)
        for c in range(4):
            up = lax.dot_general(
                recv[rows, :], wd[pl.ds(c * 256, 256), :], NT, preferred_element_type=F32
            )
            for l in range(2):
                j = 2 * c + l
                at = slice(j * 128, j * 128 + 128)
                g = up[:, l * 128 : l * 128 + 128].astype(BF16)
                g = jnp.where(bo[j, rows, :] > 0, g, jnp.zeros_like(g))
                glast[rows, at] = g
                g = g.astype(F32)
                acc[0, :, at] += folded(g)
                acc[1, :, at] += folded(g * pzd[rows, at].astype(F32))

    for group in range(4):
        project(group)

    def share(slots, own, sends, recvs, axis):
        at = me if axis == "space" else dp

        def desc(other, sender):
            return pltpu.make_async_remote_copy(
                src_ref=slots.at[at],
                dst_ref=slots.at[sender],
                send_sem=sends.at[other],
                recv_sem=recvs.at[sender],
                device_id=(other, dp) if axis == "space" else (me, other),
                device_id_type=MESH,
            )

        slots[at] = own

        for k in ORDER:
            desc(lax.rem(at + k, 16), at).start()

        def finish():
            def wait(k, carry):
                other = lax.rem(at + k, 16)
                desc(other, other).wait_recv()
                return carry

            lax.fori_loop(1, 16, wait, 0)
            return jnp.sum(slots[...], axis=0)

        def drain():
            def wait(k, carry):
                desc(lax.rem(at + k, 16), at).wait_send()
                return carry

            lax.fori_loop(1, 16, wait, 0)

        return finish, drain

    def coefficients(sums, lo, n):
        scale = gain(lo, n) * rstd(lo, n)
        crossed = sums[1:2] * rstd(lo, n)
        slope = -scale * rstd(lo, n) * crossed * (1.0 / M)
        shift = -scale * sums[0:1] * (1.0 / M)
        return scale, slope, shift, crossed

    mean1 = mean(2 * MID, CH)

    def local_sums(n, centre):
        total = jnp.sum(acc[0, :, :n], axis=0, keepdims=True)
        product = jnp.sum(acc[1, :, :n], axis=0, keepdims=True)
        return jnp.concatenate([total, product - centre * total], axis=0)

    own = local_sums(CH, mean1)
    finish1, drain1 = share(st1, own, s1s, s1r, "space")
    send_halos(zsend, zhalo, 0)
    pl.semaphore_wait(wide, 2)
    signal(other, across)

    def drain_exchange(k, carry):
        exchange(lax.rem(me + k, NS), me).wait_send()
        return carry

    lax.fori_loop(1, NS, drain_exchange, 0)
    sums1 = finish1()
    scale1, slope1, shift1, crossed1 = coefficients(sums1, 2 * MID, CH)
    shift1 = shift1 - slope1 * mean1

    acc[...] = jnp.zeros_like(acc)

    def middle(step, carry):
        rows = pl.ds(step * PLANE, PLANE)
        tiles = []
        for j in range(8):
            at = slice(j * 128, j * 128 + 128)
            z = pzd[rows, at].astype(F32)
            dz = glast[rows, at].astype(F32) * scale1[:, at] + z * slope1[:, at] + shift1[:, at]
            tiles.append(dz.astype(BF16))
            ldz[rows, at] = tiles[j]
        mi = lax.dot_general(
            jnp.concatenate(tiles, axis=1), wl[...], NT, preferred_element_type=F32
        )
        for l in range(2):
            at = slice(l * 128, l * 128 + 128)
            g = jnp.where(rm[l, rows, :].astype(F32) > 0, mi[:, at], 0.0)
            gmid[l, rows, :] = g
            acc[0, :, at] += folded(g)
            acc[1, :, at] += folded(g * zcm[l, rows, :])
        return carry

    for step in range(4):
        middle(step, 0)
    own = local_sums(MID, 0.0)
    finish2, drain2 = share(st2, own, s2s, s2r, "space")
    for slot, h in ((0, 0), (1, SLAB - 1)):
        for l in range(2):
            gsend[slot, :, l * 128 : l * 128 + 128] = gmid[
                l, pl.ds(h, PLANE, stride=SLAB), :
            ].astype(BF16)
    send_halos(gsend, ghalo, 1)
    norm_last = jnp.concatenate([crossed1, sums1[0:1]], axis=0)

    def last(step, carry):
        cols = pl.ds(step * 256, 256)
        res = jnp.dot(rmt[...], ldz[:, cols], preferred_element_type=F32)
        pflat[0, pl.ds(step, MID, stride=4), :] = res[:, :128]
        pflat[1, pl.ds(step, MID, stride=4), :] = res[:, 128:]
        return carry

    for step in range(4):
        last(step, 0)
    part[pl.ds(9 * MID, CH), :] = lanes(pflat, slice(0, CH)).astype(BF16)

    core = lax.rem(me, 2)
    chip = lax.div(me, 2)
    partner = me + 1 - 2 * core

    def block(q, c):
        return pl.ds(pl.multiple_of((2 * q + c) * SHARE, SHARE), SHARE)

    def pair(q):
        return pltpu.make_async_remote_copy(
            src_ref=part.at[block(q, 1 - core)],
            dst_ref=ra.at[q],
            send_sem=as_.at[q],
            recv_sem=ar_.at[q],
            device_id=(partner, dp),
            device_id_type=MESH,
        )

    def chips(target, sender):
        return pltpu.make_async_remote_copy(
            src_ref=sb.at[target],
            dst_ref=rb.at[sender],
            send_sem=bs_.at[target],
            recv_sem=br_.at[sender],
            device_id=(2 * target + core, dp),
            device_id_type=MESH,
        )

    def start_pairs(lo, hi):
        def go(q, carry):
            pair(q).start()
            return carry

        lax.fori_loop(lo, hi, go, 0)

    def start_chips(lo, hi):
        def go(q, carry):
            pair(q).wait_recv()
            sb[q] = (part[block(q, core), :].astype(F32) + ra[q].astype(F32)).astype(BF16)

            @pl.when(q != chip)
            def _():
                chips(q, chip).start()

            return carry

        lax.fori_loop(lo, hi, go, 0)

    start_pairs(6, 8)
    start_chips(6, 8)
    sums2 = finish2()
    scale2, slope2, shift2, crossed2 = coefficients(sums2, MID, MID)

    for l in range(2):
        at = slice(l * 128, l * 128 + 128)
        stage[l, pl.ds(8, POS), :] = (
            (gmid[l, pl.ds(0, POS), :] * scale2[:, at] + zcm[l] * slope2[:, at] + shift2[:, at])
            .astype(BF16)
            .astype(F32)
        )
    for h in range(SLAB):
        for l in range(2):
            for b in (-1, 0, 1):
                x = stage[l, pl.ds(8 + h - SLAB * b, PLANE, stride=SLAB), :]
                if b:
                    x = x * masks[(b + 1) // 2]
                lane = (b + 1) * MID + l * 128
                buf[pl.ds((h + 1) * PLANE, PLANE), lane : lane + 128] = x.astype(BF16)

    wait_halos(zsend, zhalo, 0)
    wait_halos(gsend, ghalo, 1)
    for side in range(2):
        present = me > 0 if side == 0 else me < NS - 1
        for l in range(2):
            at = slice(l * 128, l * 128 + 128)
            z = zhalo[side, :, at].astype(F32) - mean(MID + 128 * l, 128)
            dz = (
                (ghalo[side, :, at].astype(F32) * scale2[:, at] + z * slope2[:, at] + shift2[:, at])
                .astype(BF16)
                .astype(F32)
            )
            hstage[side, l, pl.ds(8, PLANE), :] = jnp.where(present, dz, 0.0)
            for b in (-1, 0, 1):
                x = hstage[side, l, pl.ds(8 - b, PLANE), :]
                if b:
                    x = x * masks[(b + 1) // 2]
                lane = (b + 1) * MID + l * 128
                buf[pl.ds(side * 5 * PLANE, PLANE), lane : lane + 128] = x.astype(BF16)


    def taps(a):
        rows = pl.ds((2 - a) * PLANE, POS)
        for b in range(3):
            part[pl.ds((3 * a + b) * MID, MID), :] = jnp.dot(
                rft[...], buf[rows, b * MID : b * MID + MID], preferred_element_type=F32
            ).astype(BF16)

    taps(0)
    start_pairs(0, 1)
    taps(1)
    start_pairs(1, 3)
    start_chips(0, 1)
    taps(2)
    start_pairs(3, 6)
    start_chips(1, 3)

    acc[...] = jnp.zeros_like(acc)
    mean3 = mean(0, MID)

    def conv(h, carry):
        total = jnp.zeros((PLANE, MID), F32)
        for a in range(3):
            rows = pl.ds((h + 2 - a) * PLANE, PLANE)
            total += lax.dot_general(buf[rows, :], wcat[a], NT, preferred_element_type=F32)
        rows = pl.ds(h * PLANE, PLANE)
        for l in range(2):
            at = slice(l * 128, l * 128 + 128)
            g = jnp.where(rfh[rows, at].astype(F32) > 0, total[:, at], 0.0)
            gfirst[l, pl.ds(h, PLANE, stride=SLAB), :] = g
            z = zfh[rows, at].astype(F32)
            acc[0, :, at] += folded(g)
            acc[1, :, at] += folded(g * z)
        return carry

    for h in range(SLAB):
        conv(h, 0)
        if h == 0:
            start_chips(3, 6)
    own = local_sums(MID, mean3)
    finish3, drain3 = share(st3, own, s3s, s3r, "space")
    pl.semaphore_wait(other, 1)
    finish_last, drain_last = share(std, norm_last, sds.at[0], sdr.at[0], "dp")
    drain1()
    drain2()

    sums3 = finish3()
    scale3, slope3, shift3, crossed3 = coefficients(sums3, 0, MID)
    own = jnp.concatenate(
        [
            jnp.concatenate([crossed3, crossed2], axis=1),
            jnp.concatenate([sums3[0:1], sums2[0:1]], axis=1),
        ],
        axis=0,
    )
    finish4, drain4 = share(st4, own, sds.at[1], sdr.at[1], "dp")
    drain3()

    for l in range(2):
        at = slice(l * 128, l * 128 + 128)
        z = pf[l].astype(F32)
        shift = shift3[:, at] - slope3[:, at] * mean3[:, at]
        ob[l] = (gfirst[l, pl.ds(0, POS), :] * scale3[:, at] + z * slope3[:, at] + shift).astype(BF16)
    outs = [
        pltpu.make_async_copy(ob4.at[l], out_hbm.at[:, :, pl.ds(l * 128, 128)], osem.at[l])
        for l in range(2)
    ]
    for copy in outs:
        copy.start()

    tc[pl.ds(0, SHARE), :] = part[block(chip, core), :].astype(F32) + ra[chip].astype(F32)

    def gather(k, carry):
        sender = lax.rem(chip + k, 8)
        chips(sender, sender).wait_recv()
        tc[pl.ds(0, SHARE), :] += rb[sender].astype(F32)
        return carry

    lax.fori_loop(1, 8, gather, 0)
    tc[pl.ds(SHARE, 8), :] = jnp.zeros((8, 256), F32)
    for d in range(ND):
        sc[d] = tc[pl.ds(d * PIECE, 16), :].astype(BF16)
    rc[dp] = sc[dp]

    def shares(target, sender):
        return pltpu.make_async_remote_copy(
            src_ref=sc.at[target],
            dst_ref=rc.at[sender],
            send_sem=cs_.at[target],
            recv_sem=cr_.at[sender],
            device_id=(me, target),
            device_id_type=MESH,
        )

    for k in ORDER:
        shares(lax.rem(dp + k, ND), dp).start()

    def drain_pairs(q, carry):
        pair(q).wait_send()

        @pl.when(q != chip)
        def _():
            chips(q, chip).wait_send()

        return carry

    lax.fori_loop(0, 8, drain_pairs, 0)

    ng_ref[:, 2 * MID :] = finish_last() * FACTOR
    drain_last()
    ng_ref[:, : 2 * MID] = finish4() * FACTOR
    drain4()

    def drain_shares(k, carry):
        shares(lax.rem(dp + k, ND), dp).wait_send()
        return carry

    lax.fori_loop(1, ND, drain_shares, 0)
    for copy in outs:
        copy.wait()

    def wait(k, carry):
        sender = lax.rem(dp + k, ND)
        shares(sender, sender).wait_recv()
        return carry

    lax.fori_loop(1, ND, wait, 0)
    mine = jnp.sum(rc[...].astype(F32), axis=0) * FACTOR
    for r in range(PIECE):
        wg_ref[2 * r : 2 * r + 1, :] = mine[r : r + 1, :128]
        wg_ref[2 * r + 1 : 2 * r + 2, :] = mine[r : r + 1, 128:]


def settle(a, b, c, x, y, z, va, vb, vc, sem):
    arrays = ((a, va, x), (b, vb, y), (c, vc, z))
    inward = [pltpu.make_async_copy(src, mid, sem.at[0, i]) for i, (src, mid, _) in enumerate(arrays)]
    outward = [pltpu.make_async_copy(mid, dst, sem.at[1, i]) for i, (_, mid, dst) in enumerate(arrays)]
    for copy in inward:
        copy.start()
    for copy, onward in zip(inward, outward):
        copy.wait()
        onward.start()
    for copy in outward:
        copy.wait()


def shards(
    deep_grad, deep_weight, pre_first, relu_first, pre_middle, relu_middle, pre_last,
    block_output, weight_middle, weight_last, norm_mean, norm_rstd, norm_gain,
):
    def turned(x):
        return jnp.transpose(x, (0, 2, 1, 3)).reshape(PLANE, SLAB, x.shape[-1])

    any_spec = pl.BlockSpec(memory_space=pl.ANY)
    vmem_spec = pl.BlockSpec(memory_space=pltpu.VMEM)
    v = lambda shape, dtype: pltpu.VMEM(shape, dtype)
    dma = lambda *shape: pltpu.SemaphoreType.DMA(shape)
    scratch = [
        v((COLS, ROWS, MID4), BF16),
        v((NS, BLOCK, MID4), BF16),
        v((POS, MID4), BF16),
        v((CH, MID4), BF16),
        v((8, PLANE, SLAB, 128), BF16),
        v((8, PLANE, SLAB, 128), BF16),
        v((2, PLANE, SLAB, 128), BF16),
        v((2, PLANE, SLAB, 128), BF16),
        v((2, PLANE, SLAB, 128), BF16),
        v((2, PLANE, SLAB, 128), BF16),
        v((MID, CH), BF16),
        v((3, MID, 3 * MID), BF16),
        v((POS, CH), BF16),
        v((POS, CH), BF16),
        v((POS, CH), BF16),
        v((2, POS, 128), F32),
        v((2, POS + 8, 128), F32),
        v((2, POS + 16, 128), F32),
        v((2, 2, PLANE + 16, 128), F32),
        v((6 * PLANE, 3 * MID), BF16),
        v((POS, MID), BF16),
        v((MID, POS), BF16),
        v((MID, POS), BF16),
        v((POS, MID), BF16),
        v((2, POS + 8, 128), F32),
        v((2, PLANE, SLAB, 128), BF16),
        v((2, 8, CH), F32),
        v((NS, 2, CH), F32),
        v((NS, 2, MID), F32),
        v((NS, 2, MID), F32),
        v((ND, 2, 2 * MID), F32),
        v((ND, 2, CH), F32),
        v((2, PLANE, MID), BF16),
        v((2, PLANE, MID), BF16),
        v((2, PLANE, MID), BF16),
        v((2, PLANE, MID), BF16),
        v((2, PLANE, 128), F32),
        v((2, CH + 8, 128), F32),
        v((FLAT, 256), BF16),
        v((8, SHARE, 256), BF16),
        v((8, SHARE, 256), BF16),
        v((8, SHARE, 256), BF16),
        v((SHARE + 8, 256), F32),
        v((ND, 16, 256), BF16),
        v((ND, 16, 256), BF16),
        dma(36), dma(4), dma(2),
        dma(16), dma(16),
        dma(16), dma(16), dma(16), dma(16), dma(16), dma(16), dma(2, 16), dma(2, 16),
        dma(2, 2), dma(2, 2),
        dma(8), dma(8), dma(8), dma(8), dma(16), dma(16),
        pltpu.SemaphoreType.REGULAR, pltpu.SemaphoreType.REGULAR, pltpu.SemaphoreType.REGULAR,
    ]
    first, weights, norms = pl.pallas_call(
        kernel,
        out_shape=(
            jax.ShapeDtypeStruct((PLANE, SLAB, MID), BF16),
            jax.ShapeDtypeStruct((2 * PIECE, 128), F32),
            jax.ShapeDtypeStruct((2, CH + 2 * MID), F32),
        ),
        in_specs=[any_spec] * 10 + [vmem_spec] * 3,
        out_specs=(any_spec, vmem_spec, vmem_spec),
        scratch_shapes=scratch,
        compiler_params=pltpu.CompilerParams(
            collective_id=0, has_side_effects=True, vmem_limit_bytes=60 << 20
        ),
    )(
        jnp.transpose(deep_grad, (0, 2, 1, 3)).reshape(COLS, ROWS, MID4),
        deep_weight,
        turned(pre_first),
        turned(relu_first),
        turned(pre_middle),
        turned(relu_middle),
        turned(pre_last),
        turned(block_output),
        weight_middle,
        weight_last,
        norm_mean,
        norm_rstd,
        norm_gain,
    )
    first, weights, norms = pl.pallas_call(
        settle,
        out_shape=tuple(jax.ShapeDtypeStruct(x.shape, x.dtype) for x in (first, weights, norms)),
        in_specs=[any_spec] * 3,
        out_specs=(any_spec,) * 3,
        scratch_shapes=[v(x.shape, x.dtype) for x in (first, weights, norms)] + [dma(2, 3)],
        compiler_params=pltpu.CompilerParams(vmem_limit_bytes=60 << 20),
    )(first, weights, norms)
    first = jnp.transpose(first.reshape(GROUP, COLS, SLAB, MID), (0, 2, 1, 3))
    return first, weights.reshape(-1), norms


def solution(mesh):
    return jax.shard_map(
        shards,
        mesh=mesh,
        in_specs=(
            P(("dp", "space"), None, None, None),
            P(),
            P("dp", "space", None, None),
            P("dp", "space", None, None),
            P("dp", "space", None, None),
            P("dp", "space", None, None),
            P("dp", "space", None, None),
            P("dp", "space", None, None),
            P(),
            P(),
            P(),
            P(),
            P(),
        ),
        out_specs=(P("dp", "space", None, None), P(("space", "dp")), P()),
        check_vma=False,
    )
```
